32 devices in a mesh: section: 2 (over core), row: 2 (over y), wide: 8 (over z, x).
Axes of the slice: x: 2, y: 2, z: 4, core: 2. Of those that a mesh axis runs over, the one named last changes fastest.
Arguments:
- inputs: bfloat16 [16, 1024, 768], P('wide', 'row'), may hold values from -6 to 6
- cotangent: bfloat16 [16, 1024, 768], P('wide', 'row'), may hold values from -6 to 6
- segment_ids: int32 [16, 1024], P('wide'), may hold values from 0 to 15, as said below
- step_number: int32 [1], replicated, may hold values from 0 to 999999
- redraw_every: int32 [1], replicated, may hold values from 1 to 1999
- bank_offset: int32 [1], replicated, may hold values from 0 to 999999
- ln1_gain: float32 [2, 768], P('section'), may hold values from 0.1 to 1.9
- ln1_bias: float32 [2, 768], P('section'), may hold values from -1.2 to 1.2
- w_qkv: bfloat16 [2, 768, 2304], P('section'), may hold values from -0.109375 to 0.109375
- b_qkv: float32 [2, 2304], P('section'), may hold values from -0.6 to 0.6
- w_out: bfloat16 [2, 768, 768], P('section'), may hold values from -0.875 to 0.875
- b_out: float32 [2, 768], P('section'), may hold values from -2 to 2
- ln2_gain: float32 [2, 768], P('section'), may hold values from 0.1 to 1.9
- ln2_bias: float32 [2, 768], P('section'), may hold values from -3 to 3
- w_up: bfloat16 [2, 768, 3072], P('section'), may hold values from -0.21875 to 0.21875
- b_up: float32 [2, 3072], P('section'), may hold values from -3 to 3
- w_down: bfloat16 [2, 3072, 768], P('section'), may hold values from -0.109375 to 0.109375
- b_down: float32 [2, 768], P('section'), may hold values from -2 to 2
- bank: float32 [2, 8, 64, 32], P('section'), may hold values from -6 to 6
Outputs:
- hidden: bfloat16 [2, 16, 1024, 768], P('section', 'wide', 'row')
- input_grads: bfloat16 [2, 16, 1024, 768], P('section', 'wide', 'row')
- grad_ln1_gain: float32 [2, 768], P('section')
- grad_ln1_bias: float32 [2, 768], P('section')
- grad_w_qkv: float32 [2, 768, 2304], P('section')
- grad_b_qkv: float32 [2, 2304], P('section')
- grad_w_out: float32 [2, 768, 768], P('section')
- grad_b_out: float32 [2, 768], P('section')
- grad_ln2_gain: float32 [2, 768], P('section')
- grad_ln2_bias: float32 [2, 768], P('section')
- grad_w_up: float32 [2, 768, 3072], P('section')
- grad_b_up: float32 [2, 3072], P('section')
- grad_w_down: float32 [2, 3072, 768], P('section')
- grad_b_down: float32 [2, 768], P('section')
The draws below stay inside these ranges and needn't reach their ends.
Inputs may be any that keep to these rules, and one draw needn't show every extreme that they name: `segment_ids`: within a sequence the ids never fall, each of 0 to 15 names one run of 1 to 128 consecutive positions, and one run has exactly 128 positions and holds positions on both sides of the sequence's middle.
All inputs are finite; a program needn't handle non-finite values.
Results may differ from the reference program's by a relative error of at most 0.02.
Values may be sent and summed in bfloat16 or wider, within the bound.
No kernel may reach another device: no remote copies, remote signals or barrier semaphores. Data moves between devices by JAX's collectives and lax.ppermute only.
A program may use at most 256 MiB of HBM per device.

```python
import math
import jax
import jax.numpy as jnp
from jax import lax

D = 768
HEADS = 12
HEAD = 64
FEATS = 32
FF = 3072
SEQ_LEN = 1024
SEGS = 16
SEG_MOST = 128
BANK = 8
SEQS = 16


def draw_segment_ids(key, part):
    key = jax.random.fold_in(key, 11)
    middle_pos = SEQ_LEN // 2
    offsets = jax.random.randint(key, (SEQS, 1), 1, SEG_MOST).astype(jnp.int32)
    places = jnp.arange(SEQ_LEN, dtype=jnp.int32)[None, :]
    start = middle_pos - offsets
    left_len = start
    right_len = SEQ_LEN - start - SEG_MOST
    lowest = jnp.maximum((left_len + SEG_MOST - 1) // SEG_MOST, SEGS - 1 - right_len)
    highest = jnp.minimum(left_len, SEGS - 1 - (right_len + SEG_MOST - 1) // SEG_MOST)
    left_count = jnp.clip((SEGS - 1) * left_len // (left_len + right_len), lowest, highest)
    right_count = SEGS - 1 - left_count
    left_ids = places * left_count // left_len
    right_ids = left_count + 1 + (places - start - SEG_MOST) * right_count // right_len
    labels = jnp.where(places < start, left_ids, jnp.where(places < start + SEG_MOST, left_count, right_ids))
    return labels.astype(jnp.int32)


def spiked(array, key, source, target, parts, factor):
    owner, partner = [(jnp.arange(array.shape[dim]) // (array.shape[dim] // parts)).reshape([-1 if axis == dim else 1 for axis in range(array.ndim)]) for dim in (source, target)]
    chosen = jax.random.permutation(key, parts)[partner]
    strong = (owner == chosen) | (owner == (partner + parts // 2) % parts)
    return jnp.where(strong, factor * array, array)


def block_levels(own_key, shape, split, low, largest):
    gain = 1.0
    for dim, shards_of in split:
        steps = jax.random.uniform(jax.random.fold_in(jax.random.fold_in(own_key, 6), dim), (shards_of,), jnp.float32, low / len(split), largest / len(split))
        gain = gain * jnp.repeat(jnp.exp(steps), shape[dim] // shards_of).reshape((-1,) + (1,) * (len(shape) - 1 - dim))
    return gain


def noise(rng, dims, deviation, most, shards=(), kind=jnp.bfloat16):
    level = block_levels(rng, dims, shards, -0.22, 0.18) if shards else 1.0
    drawn = jax.random.normal(rng, dims, jnp.float32) * deviation * level
    return jnp.minimum(jnp.maximum(drawn, -most), most).astype(kind)


def bell_draw_with(stream_key, shape, width, most, shards, heavy, kind=jnp.bfloat16):
    result = width * jax.random.normal(stream_key, shape, jnp.float32)
    if shards:
        result = result * block_levels(stream_key, shape, shards, -0.22, 0.18)
    return jnp.clip(spiked(result, jax.random.fold_in(stream_key, 3), *heavy), -most, most).astype(kind)


def setup_inputs(seed: int = 0) -> dict:
    key_list = jax.random.split(jax.random.key(seed), 20)
    inputs = noise(key_list[0], (SEQS, SEQ_LEN, D), 1.0, 6.0, ((0, 8), (1, 2)))
    cotangent = bell_draw_with(key_list[1], (SEQS, SEQ_LEN, D), 1.0, 6.0, ((0, 8), (1, 2)), (0, 2, 8, 2.0))
    segment_ids = draw_segment_ids(jax.random.fold_in(key_list[19], 71), 0)
    step_number = jax.random.randint(key_list[3], (1,), 0, 1000000).astype(jnp.int32)
    redraw_every = jax.random.randint(key_list[4], (1,), 1, 2000).astype(jnp.int32)
    bank_offset = jax.random.randint(key_list[5], (1,), 0, 1000000).astype(jnp.int32)
    ln1_gain = jnp.clip(1.0 + 0.18 * jax.random.normal(key_list[6], (2, D), jnp.float32), 0.1, 1.9)
    ln1_bias = noise(key_list[7], (2, D), 0.2, 1.2, ((0, 2),), jnp.float32)
    w_qkv = noise(key_list[8], (2, D, 3 * D), (4 * D) ** -0.5, 0.109375, ((0, 2),))
    b_qkv = noise(key_list[9], (2, 3 * D), 0.1, 0.6, ((0, 2),), jnp.float32)
    w_out = noise(key_list[10], (2, D, D), (D // 16) ** -0.5, 0.875, ((0, 2),))
    b_out = noise(key_list[11], (2, D), 0.3, 2.0, ((0, 2),), jnp.float32)
    ln2_gain = jnp.clip(1.0 + 0.18 * jax.random.normal(key_list[12], (2, D), jnp.float32), 0.1, 1.9)
    ln2_bias = noise(key_list[13], (2, D), 0.5, 3.0, ((0, 2),), jnp.float32)
    w_up = noise(key_list[14], (2, D, FF), D ** -0.5, 0.21875, ((0, 2),))
    b_up = noise(key_list[15], (2, FF), 0.5, 3.0, ((0, 2),), jnp.float32)
    w_down = noise(key_list[16], (2, FF, D), FF ** -0.5, 0.109375, ((0, 2),))
    b_down = noise(key_list[17], (2, D), 0.3, 2.0, ((0, 2),), jnp.float32)
    bank = noise(key_list[18], (2, BANK, HEAD, FEATS), 1.0, 6.0, ((0, 2),), jnp.float32)
    return dict(inputs=inputs, cotangent=cotangent, segment_ids=segment_ids, step_number=step_number, redraw_every=redraw_every, bank_offset=bank_offset, ln1_gain=ln1_gain, ln1_bias=ln1_bias, w_qkv=w_qkv, b_qkv=b_qkv, w_out=w_out, b_out=b_out, ln2_gain=ln2_gain, ln2_bias=ln2_bias, w_up=w_up, b_up=b_up, w_down=w_down, b_down=b_down, bank=bank)


precise = lax.Precision.HIGHEST
epsilon = 1e-05

@jax.custom_vjp
def low(v):
    return lax.optimization_barrier(v.astype(jnp.bfloat16)).astype(jnp.float32)

@jax.custom_vjp
def low_back(v):
    return v

def low_keep(v):
    return (low(v), None)

def low_pass(kept, grad):
    return (grad,)

def back_keep(v):
    return (v, None)

def back_low(kept, grad):
    return (low(grad),)
low.defvjp(low_keep, low_pass)
low_back.defvjp(back_keep, back_low)

def matmul(left, right):
    return jnp.dot(left, right, precision=precise, preferred_element_type=jnp.float32)

def layer_norm(values, gain_vec, offset):
    centered = values - lax.optimization_barrier(jnp.mean(values, axis=-1, keepdims=True))
    variance = lax.optimization_barrier(jnp.mean(centered * centered, axis=-1, keepdims=True))
    return centered * lax.rsqrt(variance + epsilon) * gain_vec + offset

def rotate(vectors, positions):
    halfway = vectors.shape[-1] // 2
    inverse = 10000.0 ** (-2.0 * jnp.arange(halfway, dtype=jnp.float32) / vectors.shape[-1])
    angles = positions[:, None] * inverse[None, :]
    cosine = jnp.cos(angles)[:, None, :]
    sine_part = jnp.sin(angles)[:, None, :]
    former = vectors[..., :halfway]
    latter = vectors[..., halfway:]
    return jnp.concatenate([former * cosine - latter * sine_part, latter * cosine + former * sine_part], axis=-1)

def feature_map(vectors, positions, omega):
    turned = rotate(vectors, positions) * vectors.shape[-1] ** (-0.25)
    projected = jnp.einsum('thd,dm->thm', turned, omega, precision=precise)
    squared = 0.5 * lax.optimization_barrier(jnp.sum(turned * turned, axis=-1, keepdims=True))
    return jnp.exp(projected - squared) / math.sqrt(omega.shape[-1])

def gelu_exact(values):
    return jax.nn.gelu(values, approximate=False)

def layer(weights, inputs, onehot, positions, omega):
    gain_one, bias_one, w_qkv, b_qkv, w_out, b_out, gain_two, bias_two, w_up, b_up, w_down, b_down = weights
    model_width = inputs.shape[-1]
    normed = low(layer_norm(inputs, gain_one, bias_one))
    projected = matmul(normed, w_qkv) + b_qkv
    queries = low_back(projected[:, :model_width]).reshape(-1, HEADS, HEAD)
    key_part = low_back(projected[:, model_width:2 * model_width]).reshape(-1, HEADS, HEAD)
    values = low(low_back(projected[:, 2 * model_width:])).reshape(-1, HEADS, HEAD)
    feat_q = low(feature_map(queries, positions, omega))
    feat_k = low(feature_map(key_part, positions, omega))
    seg_state = low(low_back(jnp.einsum('st,thm,thd->shmd', onehot, feat_k, values, precision=precise)))
    totals = low(low_back(jnp.einsum('st,thm->shm', onehot, feat_k, precision=precise)))
    numerator = low_back(jnp.einsum('st,thm,shmd->thd', onehot, feat_q, seg_state, precision=precise))
    denominator = low_back(jnp.einsum('st,thm,shm->th', onehot, feat_q, totals, precision=precise))
    attended = low((numerator / denominator[:, :, None]).reshape(-1, model_width))
    middle = inputs + low_back(matmul(attended, w_out) + b_out)
    normed_two = low(layer_norm(middle, gain_two, bias_two))
    up_pre = low_back(matmul(normed_two, w_up) + b_up)
    active = low(gelu_exact(up_pre))
    return middle + low_back(matmul(active, w_down) + b_down)

def reference(inputs, cotangent, segment_ids, step_number, redraw_every, bank_offset, ln1_gain, ln1_bias, w_qkv, b_qkv, w_out, b_out, ln2_gain, ln2_bias, w_up, b_up, w_down, b_down, bank):
    stacked = (ln1_gain, ln1_bias, w_qkv, b_qkv, w_out, b_out, ln2_gain, ln2_bias, w_up, b_up, w_down, b_down)
    chosen = ((bank_offset[0] + step_number[0] // redraw_every[0]) % BANK).astype(jnp.int32)
    layers = [tuple((member[layer_idx].astype(jnp.float32) for member in stacked)) for layer_idx in range(2)]
    omegas = [lax.dynamic_index_in_dim(bank[layer_idx], chosen, 0, keepdims=False).astype(jnp.float32) for layer_idx in range(2)]
    positions = jnp.arange(SEQ_LEN, dtype=jnp.float32)
    labels = jnp.arange(SEGS, dtype=jnp.int32)[:, None]

    def one_sequence(totals, pieces):
        seq_in, seq_cot, seq_ids = pieces
        onehot = (labels == seq_ids[None, :]).astype(jnp.float32)

        def first_layer(params, values):
            return layer(params, values, onehot, positions, omegas[0])

        def second_layer(params, values):
            return layer(params, values, onehot, positions, omegas[1])
        first_out, first_back = jax.vjp(first_layer, layers[0], seq_in.astype(jnp.float32))
        passed = low(first_out)
        second_out, second_back = jax.vjp(second_layer, layers[1], passed)
        grads_two, back_mid = second_back(seq_cot.astype(jnp.float32))
        mid_round = low(back_mid)
        grads_one, back_in = first_back(mid_round)
        totals = jax.tree.map(jnp.add, totals, (grads_one, grads_two))
        return (totals, (passed.astype(jnp.bfloat16), second_out.astype(jnp.bfloat16), back_in.astype(jnp.bfloat16), mid_round.astype(jnp.bfloat16)))
    initial = jax.tree.map(jnp.zeros_like, (layers[0], layers[1]))
    grad_sums, outs_seq = lax.scan(one_sequence, initial, (inputs, cotangent, segment_ids))
    hidden = jnp.stack([outs_seq[0], outs_seq[1]])
    input_grads = jnp.stack([outs_seq[2], outs_seq[3]])
    merged = [jnp.stack([grad_sums[0][layer_idx], grad_sums[1][layer_idx]]) for layer_idx in range(12)]
    return (hidden, input_grads, merged[0], merged[1], merged[2], merged[3], merged[4], merged[5], merged[6], merged[7], merged[8], merged[9], merged[10], merged[11])
```

```python
from functools import partial
import math

import jax
import jax.numpy as jnp
from jax import lax
from jax.experimental import pallas as pl
from jax.experimental.pallas import tpu as pltpu
from jax.sharding import PartitionSpec as P

HEADS = 12
HEAD = 64
FEATS = 32
EPS = 1e-05
F32 = jnp.float32
BF = jnp.bfloat16
LANES = 128
GROUP = 4
GV = GROUP * HEAD
GF = GROUP * FEATS
FCHUNK = 512
COST = 30


def dot(a, b, dims=((1,), (0,))):
    return lax.dot_general(a, b, (dims, ((), ())), preferred_element_type=F32)


def dot_t(a, b):
    return dot(a, b, ((1,), (1,)))


def tdot(a, b):
    return dot(a, b, ((0,), (0,)))


def expanded(om):
    shape = (GV, GF)
    same = (
        lax.broadcasted_iota(jnp.int32, shape, 0) // HEAD
        == lax.broadcasted_iota(jnp.int32, shape, 1) // FEATS
    )
    return jnp.where(same, jnp.concatenate([om] * GROUP, axis=0), 0.0)


def crossing(sc, ids):
    return jnp.where((ids == sc[5]) & (sc[5] == sc[6]), 1.0, 0.0)


def split(v):
    high = v.astype(BF)
    return high, (v - high.astype(F32)).astype(BF)


def norm_parts(v):
    c = v - jnp.mean(v, axis=-1, keepdims=True)
    r = lax.rsqrt(jnp.mean(c * c, axis=-1, keepdims=True) + EPS)
    return c * r, r


def norm_back(d, xhat, r, gain):
    e = d * gain
    m1 = jnp.mean(e, axis=-1, keepdims=True)
    m2 = jnp.mean(e * xhat, axis=-1, keepdims=True)
    return (e - m1 - xhat * m2) * r


def gelu_parts(x):
    z = jnp.abs(x) * (1.0 / math.sqrt(2.0))
    ex = jnp.exp(-z * z)
    t = pl.reciprocal(1.0 + 0.3275911 * z, approx=True)
    p = 0.5 * 1.061405429
    for c in (-1.453152027, 1.421413741, -0.284496736, 0.254829592):
        p = p * t + 0.5 * c
    q = p * t * ex
    return jnp.where(x < 0, q, 1.0 - q), ex


def lane_is(shape, width, k):
    return lax.broadcasted_iota(jnp.int32, shape, 1) // width == k


def half_turn(a):
    low = lax.broadcasted_iota(jnp.int32, a.shape, 1) % HEAD < HEAD // 2
    return jnp.where(low, pltpu.roll(a, 96, 1), pltpu.roll(a, 32, 1))


def block_mask(dtype):
    shape = (GF, GV)
    same = (
        lax.broadcasted_iota(jnp.int32, shape, 0) // FEATS
        == lax.broadcasted_iota(jnp.int32, shape, 1) // HEAD
    )
    return same.astype(dtype)


def squeeze_state(st):
    st = st * block_mask(F32)
    return st[0:32] + st[32:64] + st[64:96] + st[96:128]


def widen_state(st):
    return jnp.concatenate([st] * GROUP, axis=0) * block_mask(st.dtype)


def pack_kernel(*refs):
    out, at = refs[-1], 0
    for ref in refs[:-1]:
        width = ref.shape[1]
        out[:, at : at + width] = ref[...]
        at += width


def pack(arrays):
    width = sum(a.shape[1] for a in arrays)
    return pl.pallas_call(
        pack_kernel,
        grid=(1,),
        in_specs=[pl.BlockSpec(a.shape, lambda i: (0, 0)) for a in arrays],
        out_specs=pl.BlockSpec((1, width), lambda i: (0, 0)),
        out_shape=jax.ShapeDtypeStruct((1, width), F32),
        compiler_params=params(),
        cost_estimate=pl.CostEstimate(flops=10**10, bytes_accessed=10**8, transcendentals=0),
        name="pack",
    )(*arrays)


def copies(own, other, mine, at, dst, sem):
    @pl.when(mine)
    def _():
        pltpu.make_async_copy(own.at[at], dst, sem).start()

    @pl.when(jnp.logical_not(mine))
    def _():
        pltpu.make_async_copy(other.at[at], dst, sem).start()


def arrived(own, at, dst, sem):
    pltpu.make_async_copy(own.at[at], dst, sem).wait()


ANY = pl.BlockSpec(memory_space=pl.ANY)


def params(mib=60):
    return pltpu.CompilerParams(vmem_limit_bytes=mib * 1024 * 1024)


def inputs_kernel(
    sc, x, gain, bias, w, w_other, bq, cos, sin, om, idc,
    normed, u, f, vals, st, ws, oma, sqm, sems, *, layer,
):
    j = pl.program_id(0)
    d = x.shape[2]
    at = lambda i: (slice(None), pl.ds(i * d, d))

    @pl.when(j == 0)
    def _():
        for i in range(3):
            copies(w, w_other, sc[0] == layer, at(i), ws.at[i], sems.at[i])
        xhat, _ = norm_parts(x[0].astype(F32))
        normed[...] = (xhat * gain[...] + bias[...]).astype(BF)
        hi, lo = split(expanded(om[...]))
        oma[:, :GF] = hi
        oma[:, GF:] = lo
        sqm[...] = expanded(jnp.full((HEAD, GF), -0.5, F32)).astype(BF)

    for i in range(3):

        @pl.when(j == i)
        def _():
            arrived(w, at(i), ws.at[i], sems.at[i])

    @pl.when(j < 2)
    def _():
        for g in range(HEADS // GROUP):
            cols = slice(g * GV, (g + 1) * GV)
            pr = dot(normed[...], ws[j, :, cols]) + bq[:, cols]
            parts = []
            for e in range(2):
                a = pr[:, e * LANES : (e + 1) * LANES]
                parts.append(a * cos[...] + half_turn(a) * sin[...])
            turned = jnp.concatenate(parts, axis=1)
            u[0, :, cols] = turned
            uh, ul = split(turned)
            sh, sl = split(turned * turned)
            ex = dot(uh, oma[...])
            ex = ex[:, :GF] + ex[:, GF:] + dot(ul, oma[:, :GF])
            ex = ex + dot(sh, sqm[...]) + dot(sl, sqm[...])
            f[0, :, g * GF : (g + 1) * GF] = (jnp.exp(ex) * (1.0 / math.sqrt(FEATS))).astype(BF)

    @pl.when(j == 2)
    def _():
        cross = crossing(sc, idc[...]).astype(BF)
        for g in range(HEADS // GROUP):
            cols = slice(g * GV, (g + 1) * GV)
            v = (dot(normed[...], ws[2, :, cols]) + bq[:, cols]).astype(BF)
            vals[:, cols] = v
            fk = f[0, :, g * GF : (g + 1) * GF] * cross
            one = jnp.ones_like(v)
            st[:, cols] = squeeze_state(tdot(fk, v)).astype(BF)
            st[:, d + g * GV : d + (g + 1) * GV] = squeeze_state(tdot(fk, one)).astype(BF)


UNIT = 768
G1, B1, BQ, BO, G2, B2, BU, BD = 0, 1, 2, 5, 6, 7, 8, 12


def vec_at(block):
    return pl.BlockSpec((1, UNIT), lambda j, s: (0, block))


def forward_inputs(layer, sc, x, vec, w, w_other, tables, om, idc, which):
    cos, sin = tables
    t, d = x.shape[1:]
    fw = HEADS * FEATS
    c2 = lambda j, s: (0, 0)
    part = lambda j, s: (jnp.minimum(j, 1), 0, 0)
    return pl.pallas_call(
        partial(inputs_kernel, layer=layer),
        out_shape=[
            jax.ShapeDtypeStruct((t, d), BF),
            jax.ShapeDtypeStruct((2, t, d), F32),
            jax.ShapeDtypeStruct((2, t, fw), BF),
            jax.ShapeDtypeStruct((t, d), BF),
            jax.ShapeDtypeStruct((FEATS, 2 * d), BF),
        ],
        grid_spec=pltpu.PrefetchScalarGridSpec(
            num_scalar_prefetch=1,
            grid=(3,),
            in_specs=[
                pl.BlockSpec((1, t, d), which),
                vec_at(G1),
                vec_at(B1),
                ANY,
                ANY,
                pl.BlockSpec((1, UNIT), lambda j, s: (0, BQ + j)),
                pl.BlockSpec((t, LANES), c2),
                pl.BlockSpec((t, LANES), c2),
                pl.BlockSpec((HEAD, GF), c2),
                pl.BlockSpec((t, 1), c2),
            ],
            out_specs=[
                pl.BlockSpec((t, d), c2),
                pl.BlockSpec((1, t, d), part),
                pl.BlockSpec((1, t, fw), part),
                pl.BlockSpec((t, d), c2),
                pl.BlockSpec((FEATS, 2 * d), c2),
            ],
            scratch_shapes=[
                pltpu.VMEM((3, d, d), BF),
                pltpu.VMEM((GV, GV), BF),
                pltpu.VMEM((GV, GF), BF),
                pltpu.SemaphoreType.DMA((3,)),
            ],
        ),
        compiler_params=params(),
        cost_estimate=pl.CostEstimate(
            flops=COST * 20 * t * d * d, bytes_accessed=COST * (16 * t * d + 6 * d * d), transcendentals=0
        ),
        name="attention_inputs",
    )(sc, x, vec, vec, w, w_other, vec, cos, sin, om, idc)


def own_half_kernel(fq, fk, vals, idc, idr, num, den):
    t = fq.shape[1]
    same = idc[...] == idr[...]
    zero = jnp.zeros((t, LANES), BF)
    q, k = fq[0], fk[0]
    for p in range(GROUP // 2):
        v = vals[:, p * LANES : (p + 1) * LANES]
        total = None
        for e in range(2):
            fh = jnp.where(lane_is((t, GF), FEATS, 2 * p + e), q, zero)
            s = jnp.where(same, dot_t(fh, k), 0.0).astype(BF)
            mine = lane_is((t, LANES), HEAD, e)
            va = jnp.concatenate(
                [jnp.where(mine, v, zero), jnp.where(mine, jnp.ones_like(v), zero)], axis=1
            )
            more = dot(s, va)
            total = more if total is None else total + more
        num[:, p * LANES : (p + 1) * LANES] = total[:, :LANES]
        den[:, p * LANES : (p + 1) * LANES] = total[:, LANES:]


def own_half(f, vals, ids):
    idc, idr = ids
    t, d = vals.shape
    c2 = lambda g: (0, 0)
    col = lambda g: (0, g)
    return pl.pallas_call(
        own_half_kernel,
        grid=(HEADS // GROUP,),
        out_shape=[jax.ShapeDtypeStruct((t, d), F32)] * 2,
        in_specs=[
            pl.BlockSpec((1, t, GF), lambda g: (0, 0, g)),
            pl.BlockSpec((1, t, GF), lambda g: (1, 0, g)),
            pl.BlockSpec((t, GV), col),
            pl.BlockSpec((t, 1), c2),
            pl.BlockSpec((1, t), c2),
        ],
        out_specs=[pl.BlockSpec((t, GV), col)] * 2,
        compiler_params=params(),
        cost_estimate=pl.CostEstimate(flops=COST * (16 * t * t * d), bytes_accessed=COST * (12 * t * d), transcendentals=0),
        name="own_half",
    )(f, f, vals, idc, idr)


def outputs_kernel(
    sc, num, den, f, x, st, idc, bo, g2, b2, bu, bd, wo, wu, wd, wo_r, wu_r, wd_r,
    att, rden, mid, n2, act, gp, res, acc, ups, ups_too, wos, wus, wds, sems, *, layer,
):
    j = pl.program_id(0)
    steps = wus.shape[0]
    t, d = x.shape[1:]
    full = (slice(None), slice(None))
    up_at = lambda c: (slice(None), pl.ds(c * FCHUNK, FCHUNK))
    down_at = lambda c: (pl.ds(c * FCHUNK, FCHUNK), slice(None))

    @pl.when(j == 0)
    def _():
        copies(wo, wo_r, sc[0] == layer, full, wos, sems.at[0])
        for c in range(steps):
            copies(wu, wu_r, sc[0] == layer, up_at(c), wus.at[c], sems.at[1 + c])
            copies(wd, wd_r, sc[0] == layer, down_at(c), wds.at[c], sems.at[1 + steps + c])
        cross = crossing(sc, idc[...]).astype(BF)
        for g in range(HEADS // GROUP):
            cols = slice(g * GV, (g + 1) * GV)
            fqc = f[0, :, g * GF : (g + 1) * GF] * cross
            n = num[:, cols] + dot(fqc, widen_state(st[:, cols]))
            m = den[:, cols] + dot(fqc, widen_state(st[:, d + g * GV : d + (g + 1) * GV]))
            rd = 1.0 / m
            rden[:, cols] = rd
            att[:, cols] = (n * rd).astype(BF)
        arrived(wo, full, wos, sems.at[0])
        m = x[0].astype(F32) + dot(att[...], wos[...]) + bo[...]
        mid[...] = m
        xhat, _ = norm_parts(m)
        n2[...] = (xhat * g2[...] + b2[...]).astype(BF)
        acc[...] = m + bd[...]

    for c in range(steps):

        @pl.when(j == c)
        def _():
            arrived(wu, up_at(c), wus.at[c], sems.at[1 + c])

        @pl.when(j == c + 1)
        def _():
            arrived(wd, down_at(c), wds.at[c], sems.at[1 + steps + c])

    def product(into):
        into[...] = dot(n2[...], wus[jnp.minimum(j, steps - 1)]) + bu[...]

    def rest(ref):
        up = ref[...]
        phi, ex = gelu_parts(up)
        a = (up * phi).astype(BF)
        act[0] = a
        gp[...] = (phi + up * ex * (1.0 / math.sqrt(2.0 * math.pi))).astype(BF)
        acc[...] += dot(a, wds[jnp.maximum(j - 1, 0)])

    @pl.when(j == 0)
    def _():
        product(ups)

    @pl.when((j > 0) & (j < steps) & (j % 2 == 1))
    def _():
        product(ups_too)
        rest(ups)

    @pl.when((j > 0) & (j < steps) & (j % 2 == 0))
    def _():
        product(ups)
        rest(ups_too)

    @pl.when(j == steps)
    def _():
        rest(ups if steps % 2 == 1 else ups_too)
        res[...] = acc[...].astype(BF)


def forward_outputs(layer, sc, num, den, f, x, st, idc, vec, wts, which):
    wo, wu, wd = wts[:3]
    t, d = x.shape[1:]
    ff = wu.shape[1]
    steps = ff // FCHUNK
    c2 = lambda j, s: (0, 0)
    col = lambda j, s: (0, jnp.maximum(j - 1, 0))
    half_at = lambda j, s: (jnp.maximum(j - 1, 0) // (steps // 2), 0, jnp.maximum(j - 1, 0) % (steps // 2))
    ahead = BU * UNIT // FCHUNK
    return pl.pallas_call(
        partial(outputs_kernel, layer=layer),
        out_shape=[
            jax.ShapeDtypeStruct((t, d), BF),
            jax.ShapeDtypeStruct((t, d), F32),
            jax.ShapeDtypeStruct((t, d), F32),
            jax.ShapeDtypeStruct((t, d), BF),
            jax.ShapeDtypeStruct((2, t, ff // 2), BF),
            jax.ShapeDtypeStruct((t, ff), BF),
            jax.ShapeDtypeStruct((t, d), BF),
        ],
        grid_spec=pltpu.PrefetchScalarGridSpec(
            num_scalar_prefetch=1,
            grid=(steps + 1,),
            in_specs=[
                pl.BlockSpec((t, d), c2),
                pl.BlockSpec((t, d), c2),
                pl.BlockSpec((1, t, HEADS * FEATS), lambda j, s: (0, 0, 0)),
                pl.BlockSpec((1, t, d), which),
                pl.BlockSpec((FEATS, 2 * d), c2),
                pl.BlockSpec((t, 1), c2),
                vec_at(BO),
                vec_at(G2),
                vec_at(B2),
                pl.BlockSpec((1, FCHUNK), lambda j, s: (0, ahead + jnp.minimum(j, steps - 1))),
                vec_at(BD),
            ]
            + [ANY] * 6,
            out_specs=[
                pl.BlockSpec((t, d), c2),
                pl.BlockSpec((t, d), c2),
                pl.BlockSpec((t, d), c2),
                pl.BlockSpec((t, d), c2),
                pl.BlockSpec((1, t, FCHUNK), half_at),
                pl.BlockSpec((t, FCHUNK), col),
                pl.BlockSpec((t, d), c2),
            ],
            scratch_shapes=[
                pltpu.VMEM((t, d), F32),
                pltpu.VMEM((t, FCHUNK), F32),
                pltpu.VMEM((t, FCHUNK), F32),
                pltpu.VMEM((d, d), BF),
                pltpu.VMEM((steps, d, FCHUNK), BF),
                pltpu.VMEM((steps, FCHUNK, d), BF),
                pltpu.SemaphoreType.DMA((1 + 2 * steps,)),
            ],
        ),
        compiler_params=params(),
        cost_estimate=pl.CostEstimate(
            flops=COST * (4 * t * d * ff + 2 * t * d * d), bytes_accessed=COST * (4 * d * ff + 40 * t * d), transcendentals=0
        ),
        name="attention_out_and_ffn",
    )(sc, num, den, f, x, st, idc, vec, vec, vec, vec, vec, *wts)


def ffn_back_kernel(
    sc, g, gp, mid, g2, att, rden, f, idc, wd, wu, wo, wd_r, wu_r, wo_r,
    d_up, d_mid, d_br, d_num, d_den, dst, s_bd, s_bu, s_g2, s_b2, s_bo,
    acc, wos, wus, wds, sems, *, layer,
):
    j = pl.program_id(0)
    steps = wus.shape[0]
    t, d = g.shape[1:]
    full = (slice(None), slice(None))
    up_at = lambda c: (slice(None), pl.ds(c * FCHUNK, FCHUNK))
    down_at = lambda c: (pl.ds(c * FCHUNK, FCHUNK), slice(None))

    @pl.when(j == 0)
    def _():
        for c in range(steps):
            copies(wd, wd_r, sc[0] == layer, down_at(c), wds.at[c], sems.at[1 + steps + c])
            copies(wu, wu_r, sc[0] == layer, up_at(c), wus.at[c], sems.at[1 + c])
        copies(wo, wo_r, sc[0] == layer, full, wos, sems.at[0])
        acc[...] = jnp.zeros_like(acc)
        s_bd[...] = jnp.sum(g[0].astype(F32), axis=0, keepdims=True)

    for c in range(steps):

        @pl.when(j == c)
        def _():
            arrived(wu, up_at(c), wus.at[c], sems.at[1 + c])
            arrived(wd, down_at(c), wds.at[c], sems.at[1 + steps + c])

    d_act = dot_t(g[0], wds[j])
    up = (d_act * gp[...].astype(F32)).astype(BF)
    d_up[...] = up
    s_bu[...] = jnp.sum(up.astype(F32), axis=0, keepdims=True)
    acc[...] += dot_t(up, wus[j])

    @pl.when(j == pl.num_programs(0) - 1)
    def _():
        arrived(wo, full, wos, sems.at[0])
        shape = (GV, GV)
        ones = (
            lax.broadcasted_iota(jnp.int32, shape, 0) // HEAD
            == lax.broadcasted_iota(jnp.int32, shape, 1) // HEAD
        ).astype(BF)
        dn2 = acc[...]
        xhat, r = norm_parts(mid[...])
        dm = g[0].astype(F32) + norm_back(dn2, xhat, r, g2[...])
        s_g2[...] = jnp.sum(dn2 * xhat, axis=0, keepdims=True)
        s_b2[...] = jnp.sum(dn2, axis=0, keepdims=True)
        d_mid[...] = dm
        db = dm.astype(BF)
        d_br[...] = db
        s_bo[...] = jnp.sum(db.astype(F32), axis=0, keepdims=True)
        cr = crossing(sc, idc[...]).astype(BF)
        for k in range(HEADS // GROUP):
            cols = slice(k * GV, (k + 1) * GV)
            da = dot_t(db, wos[cols, :]) * rden[:, cols]
            dnb = da.astype(BF)
            d_num[:, cols] = dnb
            hi, lo = split(da * att[:, cols].astype(F32))
            ddb = (-(dot(hi, ones) + dot(lo, ones))).astype(BF)
            d_den[:, cols] = ddb
            fq = f[0, :, k * GF : (k + 1) * GF] * cr
            dst[:, cols] = squeeze_state(tdot(fq, dnb)).astype(BF)
            dst[:, d + k * GV : d + (k + 1) * GV] = squeeze_state(tdot(fq, ddb)).astype(BF)


def ffn_back(layer, sc, g, gp, mid, vec, att, rden, f, idc, wts, which):
    wu = wts[1]
    t, d = g.shape[1:]
    ff = wu.shape[1]
    steps = ff // FCHUNK
    c2 = lambda j, s: (0, 0)
    col = lambda j, s: (0, j)
    line_shape = jax.ShapeDtypeStruct((1, d), F32)
    wide = jax.ShapeDtypeStruct((t, d), BF)
    tile = pl.BlockSpec((t, d), c2)
    line = pl.BlockSpec((1, d), c2)
    return pl.pallas_call(
        partial(ffn_back_kernel, layer=layer),
        out_shape=[
            jax.ShapeDtypeStruct((t, ff), BF),
            jax.ShapeDtypeStruct((t, d), F32),
            wide,
            wide,
            wide,
            jax.ShapeDtypeStruct((FEATS, 2 * d), BF),
            line_shape,
            jax.ShapeDtypeStruct((1, ff), F32),
            line_shape,
            line_shape,
            line_shape,
        ],
        grid_spec=pltpu.PrefetchScalarGridSpec(
            num_scalar_prefetch=1,
            grid=(steps,),
            in_specs=[
                pl.BlockSpec((1, t, d), which),
                pl.BlockSpec((t, FCHUNK), col),
                tile,
                vec_at(G2),
                tile,
                tile,
                pl.BlockSpec((1, t, HEADS * FEATS), lambda j, s: (0, 0, 0)),
                pl.BlockSpec((t, 1), c2),
            ]
            + [ANY] * 6,
            out_specs=[
                pl.BlockSpec((t, FCHUNK), col),
                tile,
                tile,
                tile,
                tile,
                pl.BlockSpec((FEATS, 2 * d), c2),
                line,
                pl.BlockSpec((1, FCHUNK), col),
                line,
                line,
                line,
            ],
            scratch_shapes=[
                pltpu.VMEM((t, d), F32),
                pltpu.VMEM((d, d), BF),
                pltpu.VMEM((steps, d, FCHUNK), BF),
                pltpu.VMEM((steps, FCHUNK, d), BF),
                pltpu.SemaphoreType.DMA((1 + 2 * steps,)),
            ],
        ),
        compiler_params=params(),
        cost_estimate=pl.CostEstimate(
            flops=COST * (4 * t * d * ff + 4 * t * d * d), bytes_accessed=COST * (4 * d * ff + 40 * t * d), transcendentals=0
        ),
        name="ffn_back",
    )(sc, g, gp, mid, vec, att, rden, f, idc, *wts)


def attention_back_kernel(
    sc, f, vals, d_num, d_den, u, st, dst, idc, idr, cos, sin, om, *rest, layer
):
    t, d = vals.shape
    both_parts = len(rest) > 2
    if both_parts:
        x, gain, d_mid, w, w_other, d_proj, s_bq, d_in, s_g1, s_b1, ws, sems = rest
        fetch_weights(sc[0] == layer, w, w_other, ws, sems)
    else:
        d_proj, s_bq = rest
    hi, lo = split(expanded(om[...]))
    ones = expanded(jnp.ones((HEAD, GF), F32)).astype(BF)
    cross = crossing(sc, idc[...])
    same = idc[...] == idr[...]
    cr = cross.astype(BF)
    head_lane = lax.broadcasted_iota(jnp.int32, (t, GV), 1) % HEAD == 0
    one_lane = jnp.where(head_lane, cross, 0.0).astype(BF)

    hi_hi = jnp.concatenate([hi, hi], axis=1)
    one_one = jnp.concatenate([ones, ones], axis=1)

    for k in range(HEADS // GROUP):
        cols = slice(k * GV, (k + 1) * GV)
        tail = slice(d + k * GV, d + (k + 1) * GV)
        fcols = slice(k * GF, (k + 1) * GF)
        fq, fk = f[0, :, fcols], f[1, :, fcols]
        zf = jnp.zeros_like(fq)
        vg, dn, dd = vals[:, cols], d_num[:, cols], d_den[:, cols]
        dd1 = jnp.where(head_lane, dd, jnp.zeros_like(dd))
        state, tots = widen_state(st[:, cols]), widen_state(st[:, tail])
        d_state, d_tots = widen_state(dst[:, cols]), widen_state(dst[:, tail])
        dfq = dot_t(dn * cr, state) + dot_t(dd1 * cr, tots)
        dfk = dot_t(vg * cr, d_state) + dot_t(one_lane, d_tots)
        dv = dot(fk * cr, d_state)
        dvs = []
        for p in range(GROUP // 2):
            own = slice(p * LANES, (p + 1) * LANES)
            v1 = jnp.concatenate([vg[:, own], jnp.ones((t, LANES), BF)], axis=1)
            dvp = dv[:, own]
            for e in range(2):
                feat_lane = lane_is((t, GF), FEATS, 2 * p + e)
                mine = lane_is((t, LANES), HEAD, e)
                zero = jnp.zeros((t, LANES), BF)
                fqh, fkh = jnp.where(feat_lane, fq, zf), jnp.where(feat_lane, fk, zf)
                dnh = jnp.where(mine, dn[:, own], zero)
                ah = jnp.concatenate([dnh, jnp.where(mine, dd1[:, own], zero)], axis=1)
                pt = jnp.where(same, dot_t(ah, v1), 0.0).astype(BF)
                dfq = dfq + dot(pt, fkh)
                dfk = dfk + tdot(pt, fqh)
                pt = jnp.where(same, dot_t(fkh, fq), 0.0).astype(BF)
                dvp = dvp + dot(pt, dnh)
            dvs.append(dvp)
        parts = [jnp.concatenate(dvs, axis=1).astype(BF)]
        for q, (df, ft) in enumerate(((dfq, fq), (dfk, fk))):
            dz = df * ft.astype(F32)
            zh, zl = split(dz)
            both = jnp.concatenate([zh, zl], axis=1)
            du = dot_t(both, hi_hi) + dot_t(zh, lo) - u[q, :, cols] * dot_t(both, one_one)
            for e in range(2):
                a = du[:, e * LANES : (e + 1) * LANES]
                parts.append((a * cos[...] - half_turn(a) * sin[...]).astype(BF))
        for at, part in ((2 * d, parts[0]), (0, jnp.concatenate(parts[1:3], axis=1)), (d, jnp.concatenate(parts[3:], axis=1))):
            here = slice(at + k * GV, at + (k + 1) * GV)
            d_proj[:, here] = part
            s_bq[:, here] = jnp.sum(part.astype(F32), axis=0, keepdims=True)

    if both_parts:
        finish_inputs(d_proj, x, gain, d_mid, w, d_in, s_g1, s_b1, ws, sems)


def third(i, d):
    return (slice(None), pl.ds(i * d, d))


def fetch_weights(mine, w, w_other, ws, sems):
    for i in range(3):
        copies(w, w_other, mine, third(i, ws.shape[1]), ws.at[i], sems.at[i])


def finish_inputs(d_proj, x, gain, d_mid, w, d_in, s_g1, s_b1, ws, sems):
    d = ws.shape[1]
    dn1 = None
    for i in range(3):
        arrived(w, third(i, d), ws.at[i], sems.at[i])
        part = dot_t(d_proj[:, i * d : (i + 1) * d], ws[i])
        dn1 = part if dn1 is None else dn1 + part
    xhat, r = norm_parts(x[0].astype(F32))
    d_in[...] = (d_mid[...] + norm_back(dn1, xhat, r, gain[...])).astype(BF)
    s_g1[...] = jnp.sum(dn1 * xhat, axis=0, keepdims=True)
    s_b1[...] = jnp.sum(dn1, axis=0, keepdims=True)


def inputs_back_kernel(sc, d_proj, x, gain, d_mid, w, w_other, d_in, s_g1, s_b1, ws, sems, *, layer):
    fetch_weights(sc[0] == layer, w, w_other, ws, sems)
    finish_inputs(d_proj, x, gain, d_mid, w, d_in, s_g1, s_b1, ws, sems)


def whole(a):
    return pl.BlockSpec(a.shape, lambda j, s: (0,) * len(a.shape))


def input_specs(d_mid, which):
    t, d = d_mid.shape
    shapes = [
        jax.ShapeDtypeStruct((t, d), BF),
        jax.ShapeDtypeStruct((1, d), F32),
        jax.ShapeDtypeStruct((1, d), F32),
    ]
    specs = [pl.BlockSpec((1, t, d), which), vec_at(G1), whole(d_mid), ANY, ANY]
    return shapes, specs, [pltpu.VMEM((3, d, d), BF), pltpu.SemaphoreType.DMA((3,))]


def attention_back(layer, sc, f, vals, d_num, d_den, u, st, dst, ids, tables, om, inputs):
    t, d = vals.shape
    operands = [f, vals, d_num, d_den, u, st, dst, *ids, *tables, om]
    specs = [whole(a) for a in operands]
    shapes = [jax.ShapeDtypeStruct((t, 3 * d), BF), jax.ShapeDtypeStruct((1, 3 * d), F32)]
    scratch = []
    if inputs is not None:
        x, vec, d_mid, w, w_other, which = inputs
        more, more_specs, scratch = input_specs(d_mid, which)
        operands += [x, vec, d_mid, w, w_other]
        specs += more_specs
        shapes += more
    return pl.pallas_call(
        partial(attention_back_kernel, layer=layer),
        out_shape=shapes,
        grid_spec=pltpu.PrefetchScalarGridSpec(
            num_scalar_prefetch=1,
            grid=(1,),
            in_specs=specs,
            out_specs=[whole(a) for a in shapes],
            scratch_shapes=scratch,
        ),
        compiler_params=params(),
        cost_estimate=pl.CostEstimate(
            flops=COST * 48 * t * t * d, bytes_accessed=COST * 40 * t * d, transcendentals=0
        ),
        name="attention_back",
    )(sc, *operands)


def inputs_back(layer, sc, d_proj, x, vec, d_mid, w, w_other, which):
    t, d = d_mid.shape
    shapes, specs, scratch = input_specs(d_mid, which)
    return pl.pallas_call(
        partial(inputs_back_kernel, layer=layer),
        out_shape=shapes,
        grid_spec=pltpu.PrefetchScalarGridSpec(
            num_scalar_prefetch=1,
            grid=(1,),
            in_specs=[whole(d_proj)] + specs,
            out_specs=[whole(a) for a in shapes],
            scratch_shapes=scratch,
        ),
        compiler_params=params(),
        cost_estimate=pl.CostEstimate(
            flops=COST * 6 * t * d * d, bytes_accessed=COST * 16 * t * d, transcendentals=0
        ),
        name="inputs_back",
    )(sc, d_proj, x, vec, d_mid, w, w_other)


ROWS = UNIT // 2


def weight_grad_kernel(sc, *refs, sizes, dims):
    send, keep = refs[-2:]
    at = 0
    for m, size in enumerate(sizes):
        left, left_r, right, right_r = refs[4 * m : 4 * m + 4]

        @pl.when((pl.program_id(0) >= at) & (pl.program_id(0) < at + size))
        def _():
            total = tdot(left[0], right[0]) + tdot(left_r[0], right_r[0])
            low, high = total[:, :ROWS].astype(BF), total[:, ROWS:].astype(BF)

            @pl.when(bit_of(sc, dims) == 0)
            def _():
                keep[0] = low
                send[0] = high

            @pl.when(bit_of(sc, dims) == 1)
            def _():
                keep[0] = high
                send[0] = low

        at += size


def weight_grad(sc, members, dims):
    sizes = [m[-1] for m in members]
    operands, specs, at = [], [], 0
    for left, lp, left_r, lrp, right, rp, right_r, rrp, size in members:
        t = left.shape[1]
        here = lambda i, at=at, size=size: jnp.clip(i - at, 0, size - 1)
        operands += [left, left_r, right, right_r]
        specs += [
            pl.BlockSpec((1, t, ROWS), lambda i, s, f=lp, h=here: f(h(i), s[0])),
            pl.BlockSpec((1, t, ROWS), lambda i, s, f=lrp, h=here: f(h(i), s[0])),
            pl.BlockSpec((1, t, UNIT), lambda i, s, f=rp, h=here: f(h(i), s[0])),
            pl.BlockSpec((1, t, UNIT), lambda i, s, f=rrp, h=here: f(h(i), s[0])),
        ]
        at += size
    shape = jax.ShapeDtypeStruct((at, ROWS, ROWS), BF)
    spec = pl.BlockSpec((1, ROWS, ROWS), lambda i, s: (i, 0, 0))
    return pl.pallas_call(
        partial(weight_grad_kernel, sizes=sizes, dims=dims),
        out_shape=[shape, shape],
        grid_spec=pltpu.PrefetchScalarGridSpec(
            num_scalar_prefetch=1, grid=(at,), in_specs=specs, out_specs=[spec, spec]
        ),
        compiler_params=params(),
        cost_estimate=pl.CostEstimate(
            flops=COST * 2 * at * t * UNIT * UNIT, bytes_accessed=COST * at * 4 * t * UNIT, transcendentals=0
        ),
        name="weight_grad",
    )(sc, *operands)


def chip_bits():
    wide, row = lax.axis_index("wide"), lax.axis_index("row")
    return {"x": wide % 2, "y": row, "z0": wide // 2 % 2, "z1": wide // 4}


def bit_of(sc, dims):
    if dims is None:
        return 0
    at = [1 + ("x", "y", "z0", "z1").index(d) for d in dims]
    return jnp.where(sc[0] == 0, sc[at[0]], sc[at[1]])


class Links:
    def __init__(self):
        self.section = lax.axis_index("section")
        self.bits = chip_bits()

    def bit(self, dims):
        return jnp.where(self.section == 0, self.bits[dims[0]], self.bits[dims[1]])

    def swap(self, value, dims):
        flips = {"x": (0, 1), "y": (1, 0), "z0": (0, 2), "z1": (0, 4)}
        pairs = []
        for s in range(2):
            fr, fw = flips[dims[s]]
            for r in range(2):
                for w in range(8):
                    pairs.append(((s * 2 + r) * 8 + w, (s * 2 + (r ^ fr)) * 8 + (w ^ fw)))
        return lax.ppermute(value, ("section", "row", "wide"), pairs)


AXES = {"x": "x", "y": "y", "z": "z0", "w": "z1"}


def pick(parts, bit):
    total = None
    for p in parts:
        one = lax.dynamic_index_in_dim(p, bit, 0, keepdims=False).astype(F32)
        total = one if total is None else total + one
    return total.astype(BF)


def add(parts):
    return parts[0] + parts[1]


def join(own, other, bit):
    return jnp.stack([jnp.where(bit == 0, own, other), jnp.where(bit == 0, other, own)])


def fence_kernel(token, out):
    pass


def fence(token, values):
    (token,) = after([token], values)
    return pl.pallas_call(
        fence_kernel,
        out_shape=jax.ShapeDtypeStruct(token.shape, token.dtype),
        in_specs=[pl.BlockSpec(memory_space=pl.ANY)],
        out_specs=pl.BlockSpec(memory_space=pl.ANY),
        input_output_aliases={0: 0},
        compiler_params=params(1),
        cost_estimate=pl.CostEstimate(flops=10**12, bytes_accessed=10**9, transcendentals=0),
        name="fence",
    )(token)


def scattered_sum(value):
    part = lax.psum_scatter(value, ("row", "wide"), scatter_dimension=0, tiled=True)
    return lax.all_gather(part, ("row", "wide"), axis=0, tiled=True)


def after(values, others):
    values, others = list(values), list(others)
    if not others:
        return values
    return list(lax.optimization_barrier(tuple(values + others)))[: len(values)]


SWAP = [(0, 1), (1, 0)]


class Flow:
    def __init__(self, links, kinds, owner):
        self.links, self.owner = links, owner
        self.step = 0
        self.order = None if links is None else [tuple(AXES[a] for a in dims) for dims in zip(*kinds)]

    def first_dims(self):
        return None if self.links is None else self.order[0]

    def begin(self, send, keep):
        self.shape = send.shape
        self.parts = keep
        if self.links is None:
            self.flight = send
        else:
            self.flight = self.links.swap(send, self.order[0])

    def advance(self, others=()):
        (came,) = after([self.flight], others)
        self.step += 1
        step = self.step
        if self.links is None:
            return self.plain(came)
        if step == 6:
            self.flight = self.over(came)
            self.mine = (self.parts, came)
            return [came]
        if step == 7:
            (early,) = after([self.early], others)
            self.result = (*self.mine, early, came)
            return [came, early]
        if step == 1:
            shape = (2, self.shape[0] * self.shape[1] // 2, self.shape[2])
            self.parts = [self.parts.reshape(shape), came.reshape(shape)]
            dims = self.order[1]
            send = pick(self.parts, 1 - self.links.bit(dims))
        elif step == 2:
            dims = self.order[2]
            send = self.parts = add([pick(self.parts, self.links.bit(self.order[1])), came])
        elif step == 3:
            dims = self.order[3]
            send = self.parts = add([self.parts, came])
        elif step == 4:
            dims = self.order[1]
            send = self.parts = add([self.parts, came])
        else:
            dims = self.order[0]
            send = self.parts = join(self.parts, came, self.links.bit(self.order[1])).reshape(self.shape)
        self.flight = self.links.swap(send, dims)
        if step == 5:
            self.early = self.over(send)
        return [send]

    def over(self, value):
        return lax.ppermute(value, "section", [(1 - self.owner, self.owner)])

    def plain(self, came):
        total = jnp.concatenate([self.parts, came], axis=0)
        mine = scattered_sum(total.reshape(-1, ROWS)).reshape((2,) + self.shape)
        self.result = (mine[0], mine[1], self.over(mine[0]), self.over(mine[1]))
        return []


def finish_kernel(sc, *refs, by_row, dims):
    out = refs[-1]
    for layer in range(2):
        for side in range(2):
            half = layer if side == 0 else 1 - layer
            base = 0 if by_row else half * ROWS
            ends = dims[layer] if side == 0 or dims[layer] is None else dims[layer][::-1]
            for bit in range(2):
                here = (sc[0] == layer) & (bit_of(sc, ends) == bit)
                if by_row:
                    here = here & (pl.program_id(1) == half)

                @pl.when(here)
                def _():
                    at = 4 * layer + 2 * side
                    out[base : base + ROWS, :ROWS] = refs[at + bit][0].astype(F32)
                    out[base : base + ROWS, ROWS:] = refs[at + 1 - bit][0].astype(F32)


def finish(sc, first, second, start, units, by_row, dims):
    spec = lambda layer: pl.BlockSpec(
        (1, ROWS, ROWS), lambda u, h, s: (start + jnp.where(s[0] == layer, u, 0), 0, 0)
    )
    if by_row:
        shape, grid = (2 * units * ROWS, UNIT), (units, 2)
        out = pl.BlockSpec((ROWS, UNIT), lambda u, h, s: (h * units + u, 0))
    else:
        shape, grid = (UNIT, units * UNIT), (units, 1)
        out = pl.BlockSpec((UNIT, UNIT), lambda u, h, s: (0, u))
    return pl.pallas_call(
        partial(finish_kernel, by_row=by_row, dims=dims),
        out_shape=jax.ShapeDtypeStruct(shape, F32),
        grid_spec=pltpu.PrefetchScalarGridSpec(
            num_scalar_prefetch=1,
            grid=grid,
            in_specs=[spec(0)] * 4 + [spec(1)] * 4,
            out_specs=out,
        ),
        compiler_params=params(),
        cost_estimate=pl.CostEstimate(
            flops=COST * units * UNIT * UNIT, bytes_accessed=COST * units * 8 * UNIT * UNIT, transcendentals=0
        ),
        name="finish",
    )(sc, *first, *second)[None]


def local(
    inputs, cotangent, segment_ids, step_number, redraw_every, bank_offset,
    ln1_gain, ln1_bias, w_qkv, b_qkv, w_out, b_out, ln2_gain, ln2_bias,
    w_up, b_up, w_down, b_down, bank,
):
    section = lax.axis_index("section")
    row = lax.axis_index("row")
    first = section == 0
    t, d = inputs.shape[1:]
    ff = w_up.shape[2]
    swap = [(0, 1), (1, 0)]

    def both(own):
        other = lax.ppermute(own, "section", swap)
        return own, other

    w_qkv, w_qkv_r = both(w_qkv[0])
    chosen = (bank_offset[0] + step_number[0] // redraw_every[0]) % bank.shape[1]
    omega = lax.dynamic_index_in_dim(bank[0], chosen, 0, keepdims=False)
    vectors = pack([ln1_gain, ln1_bias, b_qkv, b_out, ln2_gain, ln2_bias, b_up, b_down])
    vectors_r = lax.ppermute(vectors, "section", swap)
    omega, omega_r = both(jnp.concatenate([omega] * GROUP, axis=1))
    w_out, w_out_r = both(w_out[0])
    w_up, w_up_r = both(w_up[0])
    w_down, w_down_r = both(w_down[0])

    lane = lax.broadcasted_iota(jnp.int32, (t, LANES), 1) % HEAD
    place = (row * t + lax.broadcasted_iota(jnp.int32, (t, LANES), 0)).astype(F32)
    angles = place * (10000.0 ** (-2.0 * (lane % (HEAD // 2)).astype(F32) / HEAD))
    scale = HEAD ** (-0.25)
    tables = (jnp.cos(angles) * scale, jnp.sin(angles) * jnp.where(lane < HEAD // 2, -scale, scale))

    own_ids = lax.dynamic_slice(segment_ids, (section, row * t), (1, t))
    edge = lax.dynamic_slice(segment_ids, (section, jnp.int32(t - 1)), (1, 2))[0]
    ids = (own_ids.reshape(t, 1), own_ids)
    other_row = [(i, i ^ 1) for i in range(2)]
    by_section = lambda j, s: (s[0], 0, 0)
    only = lambda j, s: (0, 0, 0)

    sc = jnp.concatenate([jnp.stack([section, *chip_bits().values()]), edge]).astype(jnp.int32)
    saved, given = [], []
    x, which = inputs, by_section
    for layer in range(2):
        mine = section == layer
        vec = jnp.where(mine, vectors, vectors_r)
        om = jnp.where(mine, omega, omega_r)
        normed, u, f, vals, st = forward_inputs(layer, sc, x, vec, w_qkv, w_qkv_r, tables, om, ids[0], which)
        st = lax.ppermute(st, "row", other_row)
        num, den = own_half(f, vals, ids)
        att, rden, mid, n2, act, gp, res = forward_outputs(
            layer, sc, num, den, f, x, st, ids[0], vec, (w_out, w_up, w_down, w_out_r, w_up_r, w_down_r), which
        )
        saved.append((sc, x, vec, om, which, normed, u, f, vals, st, att, rden, mid, n2, act, gp))
        x, which = res[None], only
        given.append([lax.ppermute(g, "section", swap) for g in (n2, att, normed, act)])
    outs = (saved[1][1][0], x[0])

    def to_owner(of_layer):
        mine = jnp.where(first, of_layer[0], of_layer[1])
        other = lax.ppermute(jnp.where(first, of_layer[1], of_layer[0]), "section", swap)
        return join(mine, other, section)[None]

    hidden = to_owner(outs)

    links = Links() if lax.axis_size("wide") == 8 else None
    flows = {
        name + str(layer): Flow(links, KINDS[name + str(layer)], layer)
        for layer in range(2)
        for name in "duq"
    }
    at_own = lambda i, s: (s, 0, 0)
    at_other = lambda i, s: (1 - s, 0, 0)
    at_first = lambda i, s: (0, 0, 0)
    at_unit = lambda i, s: (0, 0, i)
    grads = {1: (cotangent, at_own, cotangent, at_other)}
    parts, back, done = {}, {}, {}
    shown = []

    def tied(value):
        (value,) = after([value], shown)
        shown.clear()
        return value

    def members(name):
        layer = int(name[1])
        normed, att, n2, act = (saved[layer][i] for i in (5, 10, 13, 14))
        gave_n2, gave_att, gave_normed, gave_act = given[layer]
        if name[0] == "d":
            left = (act, lambda i, s: (s, 0, i), gave_act, lambda i, s: (s, 0, i))
            return [(*left, *grads[layer], ff // UNIT)]

        def one(own, other, right, units):
            return (
                own[None], lambda i, s: (0, 0, s), other[None], lambda i, s: (0, 0, s),
                right[0][None], at_unit, right[1][None], at_unit, units,
            )

        if name[0] == "u":
            return [
                one(n2, gave_n2, done["up", layer], ff // UNIT),
                one(att, gave_att, done["br", layer], 1),
            ]
        return [one(normed, gave_normed, done["proj", layer], 3)]

    def run(item):
        name, layer = item[:2], int(item[1])
        if name in flows and len(item) == 2:
            before = list(shown)
            shown.clear()
            shown.extend(flows[name].advance(before))
        elif name in flows:
            send, keep = weight_grad(tied(sc), members(name), flows[name].first_dims())
            shown.append(send)
            flows[name].begin(send, keep)
        elif name[0] == "f":
            _, x, vec, om, which, normed, u, f, vals, st, att, rden, mid, n2, act, gp = saved[layer]
            g = grads[layer][0]
            back[layer] = ffn_back(
                layer, sc, g, tied(gp), mid, vec, att, rden, f, ids[0],
                (w_down, w_up, w_out, w_down_r, w_up_r, w_out_r),
                by_section if layer == 1 else only,
            )
            shown.append(back[layer][0])
            done["dst", layer] = lax.ppermute(back[layer][5], "row", other_row)
            done["up", layer] = both(back[layer][0])
            done["br", layer] = both(back[layer][2])
        elif name[0] == "a":
            _, x, vec, om, which, normed, u, f, vals, st = saved[layer][:10]
            d_mid, _, d_num, d_den = back[layer][1:5]
            out = attention_back(
                layer, sc, f, vals, tied(d_num), d_den, u, st, done["dst", layer], ids, tables, om,
                (x, vec, d_mid, w_qkv, w_qkv_r, which) if layer == 1 else None,
            )
            shown.append(out[0])
            done["proj", layer] = both(out[0])
            parts[layer] = out[1]
            if layer == 1:
                done["in", 1] = out[2:]
                own, other = both(out[2])
                grads[0] = (own[None], at_first, other[None], at_first)
        elif name[0] == "i":
            _, x, vec, om, which = saved[layer][:5]
            done["in", 0] = inputs_back(
                layer, sc, tied(done["proj", 0][0]), x, vec, back[0][1], w_qkv, w_qkv_r, which
            )
            shown.append(done["in", 0][0])
        elif name[0] == "s":
            smalls = []
            for k in range(2):
                s_bd, s_bu, s_g2, s_b2, s_bo = back[k][6:]
                smalls += [*done["in", k][1:], parts[k], s_bo, s_g2, s_b2, s_bu, s_bd]
            done["small"] = lax.psum(tied(pack(smalls)), ("section", "row", "wide"))
        else:
            kind, start, units, by_row = MATRICES[name]
            firsts, seconds = flows[kind + "0"].result, flows[kind + "1"].result
            dims = [flows[kind + str(k)].first_dims() for k in range(2)]
            done[name] = finish(tied(sc), firsts, seconds, start, units, by_row, dims)
            shown.append(done[name])

    token, fenced = jnp.zeros((8, LANES), F32), False
    for item in ORDER if links is not None else PLAIN:
        run(item)
        fenced = fenced or item == LAST
        if fenced and links is not None:
            token = fence(token, shown)
            shown[:] = [token]
    both_layers = done["small"].reshape(2, -1) + token[:1, :1]
    small = lax.dynamic_slice_in_dim(both_layers, section, 1)
    input_grads = to_owner((done["in", 0][0], done["in", 1][0]))
    g1, b1, bq, bo, gain2, bias2, bu, bd = cut(small, d, ff)
    return (
        hidden, input_grads, g1, b1, done["m0"], bq, done["m1"], bo,
        gain2, bias2, done["m2"], bu, done["m3"], bd,
    )


MATRICES = {"m0": ("q", 0, 3, False), "m1": ("u", 4, 1, False), "m2": ("u", 0, 4, False), "m3": ("d", 0, 4, True)}

KINDS = {
    "d1": ("yxwz", "xyzw"),
    "u1": ("xzwy", "zywx"),
    "q1": ("wyxz", "yxzw"),
    "d0": ("yxzw", "xywz"),
    "u0": ("xyzw", "yxwz"),
    "q0": ("yxwz", "xyzw"),
}

ORDER = (
    "f1", "d1w", "a1", "d1", "u1w", "d1", "d0w", "f0", "d0", "d1", "q1w", "d0", "a0", "u1", "u0w", "d0", "u1",
    "q0w", "q1", "u0", "i0", "d1", "q0", "q1", "u0", "d0", "s0", "d1", "q1", "d0", "u0", "u1", "d1", "q0",
    "q1", "d0", "u1", "u0", "q0", "u1", "q1", "u0", "q0", "d1", "d0", "m3", "q0", "u1", "u0", "q1", "u1",
    "u0", "m1", "q1", "q0", "m2", "q0", "m0",
)

LAST = "i0"

PLAIN = (
    "d1w", "d1", "f1", "u1w", "u1", "a1", "q1w", "q1", "d0w", "d0", "f0", "u0w", "u0", "a0", "q0w", "q0",
    "i0", "s0", "m3", "m2", "m1", "m0",
)


def cut(vec, d, ff):
    out, at = [], 0
    for size in (d, d, 3 * d, d, d, d, ff, d):
        out.append(vec[:, at : at + size])
        at += size
    return out


def solution(mesh):
    return jax.shard_map(
        local,
        mesh=mesh,
        in_specs=(
            P("wide", "row", None),
            P("wide", "row", None),
            P("wide", None),
            P(),
            P(),
            P(),
            P("section", None),
            P("section", None),
            P("section", None, None),
            P("section", None),
            P("section", None, None),
            P("section", None),
            P("section", None),
            P("section", None),
            P("section", None, None),
            P("section", None),
            P("section", None, None),
            P("section", None),
            P("section", None, None, None),
        ),
        out_specs=(
            P("section", "wide", "row", None),
            P("section", "wide", "row", None),
            P("section", None),
            P("section", None),
            P("section", None, None),
            P("section", None),
            P("section", None, None),
            P("section", None),
            P("section", None),
            P("section", None),
            P("section", None, None),
            P("section", None),
            P("section", None, None),
            P("section", None),
        ),
        check_vma=False,
    )
```

```python
from functools import partial
import math

import jax
import jax.numpy as jnp
from jax import lax
from jax.experimental import pallas as pl
from jax.experimental.pallas import tpu as pltpu
from jax.sharding import PartitionSpec as P

HEADS = 12
HEAD = 64
FEATS = 32
EPS = 1e-05
F32 = jnp.float32
BF = jnp.bfloat16
LANES = 128
GROUP = 4
GV = GROUP * HEAD
GF = GROUP * FEATS
FCHUNK = 512
COST = 30


def dot(a, b, dims=((1,), (0,))):
    return lax.dot_general(a, b, (dims, ((), ())), preferred_element_type=F32)


def dot_t(a, b):
    return dot(a, b, ((1,), (1,)))


def tdot(a, b):
    return dot(a, b, ((0,), (0,)))


def expanded(om):
    shape = (GV, GF)
    same = (
        lax.broadcasted_iota(jnp.int32, shape, 0) // HEAD
        == lax.broadcasted_iota(jnp.int32, shape, 1) // FEATS
    )
    return jnp.where(same, jnp.concatenate([om] * GROUP, axis=0), 0.0)


def crossing(sc, ids):
    return jnp.where((ids == sc[5]) & (sc[5] == sc[6]), 1.0, 0.0)


def split(v):
    high = v.astype(BF)
    return high, (v - high.astype(F32)).astype(BF)


def norm_parts(v):
    c = v - jnp.mean(v, axis=-1, keepdims=True)
    r = lax.rsqrt(jnp.mean(c * c, axis=-1, keepdims=True) + EPS)
    return c * r, r


def norm_back(d, xhat, r, gain):
    e = d * gain
    m1 = jnp.mean(e, axis=-1, keepdims=True)
    m2 = jnp.mean(e * xhat, axis=-1, keepdims=True)
    return (e - m1 - xhat * m2) * r


def gelu_parts(x):
    z = jnp.abs(x) * (1.0 / math.sqrt(2.0))
    ex = jnp.exp(-z * z)
    t = pl.reciprocal(1.0 + 0.3275911 * z, approx=True)
    p = 0.5 * 1.061405429
    for c in (-1.453152027, 1.421413741, -0.284496736, 0.254829592):
        p = p * t + 0.5 * c
    q = p * t * ex
    return jnp.where(x < 0, q, 1.0 - q), ex


def lane_is(shape, width, k):
    return lax.broadcasted_iota(jnp.int32, shape, 1) // width == k


def half_turn(a):
    low = lax.broadcasted_iota(jnp.int32, a.shape, 1) % HEAD < HEAD // 2
    return jnp.where(low, pltpu.roll(a, 96, 1), pltpu.roll(a, 32, 1))


def block_mask(dtype):
    shape = (GF, GV)
    same = (
        lax.broadcasted_iota(jnp.int32, shape, 0) // FEATS
        == lax.broadcasted_iota(jnp.int32, shape, 1) // HEAD
    )
    return same.astype(dtype)


def squeeze_state(st):
    st = st * block_mask(F32)
    return st[0:32] + st[32:64] + st[64:96] + st[96:128]


def widen_state(st):
    return jnp.concatenate([st] * GROUP, axis=0) * block_mask(st.dtype)


def pack_kernel(*refs):
    out, at = refs[-1], 0
    for ref in refs[:-1]:
        width = ref.shape[1]
        out[:, at : at + width] = ref[...]
        at += width


def pack(arrays):
    width = sum(a.shape[1] for a in arrays)
    return pl.pallas_call(
        pack_kernel,
        grid=(1,),
        in_specs=[pl.BlockSpec(a.shape, lambda i: (0, 0)) for a in arrays],
        out_specs=pl.BlockSpec((1, width), lambda i: (0, 0)),
        out_shape=jax.ShapeDtypeStruct((1, width), F32),
        compiler_params=params(),
        cost_estimate=pl.CostEstimate(flops=10**10, bytes_accessed=10**8, transcendentals=0),
        name="pack",
    )(*arrays)


def copies(own, other, mine, at, dst, sem):
    @pl.when(mine)
    def _():
        pltpu.make_async_copy(own.at[at], dst, sem).start()

    @pl.when(jnp.logical_not(mine))
    def _():
        pltpu.make_async_copy(other.at[at], dst, sem).start()


def arrived(own, at, dst, sem):
    pltpu.make_async_copy(own.at[at], dst, sem).wait()


ANY = pl.BlockSpec(memory_space=pl.ANY)


def params(mib=60):
    return pltpu.CompilerParams(vmem_limit_bytes=mib * 1024 * 1024)


def inputs_kernel(
    sc, x, gain, bias, w, w_other, bq, cos, sin, om, idc,
    normed, u, f, vals, st, ws, oma, sqm, sems, *, layer,
):
    j = pl.program_id(0)
    d = x.shape[2]
    at = lambda i: (slice(None), pl.ds(i * d, d))

    @pl.when(j == 0)
    def _():
        for i in range(3):
            copies(w, w_other, sc[0] == layer, at(i), ws.at[i], sems.at[i])
        xhat, _ = norm_parts(x[0].astype(F32))
        normed[...] = (xhat * gain[...] + bias[...]).astype(BF)
        hi, lo = split(expanded(om[...]))
        oma[:, :GF] = hi
        oma[:, GF:] = lo
        sqm[...] = expanded(jnp.full((HEAD, GF), -0.5, F32)).astype(BF)

    for i in range(3):

        @pl.when(j == i)
        def _():
            arrived(w, at(i), ws.at[i], sems.at[i])

    @pl.when(j < 2)
    def _():
        for g in range(HEADS // GROUP):
            cols = slice(g * GV, (g + 1) * GV)
            pr = dot(normed[...], ws[j, :, cols]) + bq[:, cols]
            parts = []
            for e in range(2):
                a = pr[:, e * LANES : (e + 1) * LANES]
                parts.append(a * cos[...] + half_turn(a) * sin[...])
            turned = jnp.concatenate(parts, axis=1)
            u[0, :, cols] = turned
            uh, ul = split(turned)
            sh, sl = split(turned * turned)
            ex = dot(uh, oma[...])
            ex = ex[:, :GF] + ex[:, GF:] + dot(ul, oma[:, :GF])
            ex = ex + dot(sh, sqm[...]) + dot(sl, sqm[...])
            f[0, :, g * GF : (g + 1) * GF] = (jnp.exp(ex) * (1.0 / math.sqrt(FEATS))).astype(BF)

    @pl.when(j == 2)
    def _():
        cross = crossing(sc, idc[...]).astype(BF)
        for g in range(HEADS // GROUP):
            cols = slice(g * GV, (g + 1) * GV)
            v = (dot(normed[...], ws[2, :, cols]) + bq[:, cols]).astype(BF)
            vals[:, cols] = v
            fk = f[0, :, g * GF : (g + 1) * GF] * cross
            one = jnp.ones_like(v)
            st[:, cols] = squeeze_state(tdot(fk, v)).astype(BF)
            st[:, d + g * GV : d + (g + 1) * GV] = squeeze_state(tdot(fk, one)).astype(BF)


UNIT = 768
G1, B1, BQ, BO, G2, B2, BU, BD = 0, 1, 2, 5, 6, 7, 8, 12


def vec_at(block):
    return pl.BlockSpec((1, UNIT), lambda j, s: (0, block))


def forward_inputs(layer, sc, x, vec, w, w_other, tables, om, idc, which):
    cos, sin = tables
    t, d = x.shape[1:]
    fw = HEADS * FEATS
    c2 = lambda j, s: (0, 0)
    part = lambda j, s: (jnp.minimum(j, 1), 0, 0)
    return pl.pallas_call(
        partial(inputs_kernel, layer=layer),
        out_shape=[
            jax.ShapeDtypeStruct((t, d), BF),
            jax.ShapeDtypeStruct((2, t, d), F32),
            jax.ShapeDtypeStruct((2, t, fw), BF),
            jax.ShapeDtypeStruct((t, d), BF),
            jax.ShapeDtypeStruct((FEATS, 2 * d), BF),
        ],
        grid_spec=pltpu.PrefetchScalarGridSpec(
            num_scalar_prefetch=1,
            grid=(3,),
            in_specs=[
                pl.BlockSpec((1, t, d), which),
                vec_at(G1),
                vec_at(B1),
                ANY,
                ANY,
                pl.BlockSpec((1, UNIT), lambda j, s: (0, BQ + j)),
                pl.BlockSpec((t, LANES), c2),
                pl.BlockSpec((t, LANES), c2),
                pl.BlockSpec((HEAD, GF), c2),
                pl.BlockSpec((t, 1), c2),
            ],
            out_specs=[
                pl.BlockSpec((t, d), c2),
                pl.BlockSpec((1, t, d), part),
                pl.BlockSpec((1, t, fw), part),
                pl.BlockSpec((t, d), c2),
                pl.BlockSpec((FEATS, 2 * d), c2),
            ],
            scratch_shapes=[
                pltpu.VMEM((3, d, d), BF),
                pltpu.VMEM((GV, GV), BF),
                pltpu.VMEM((GV, GF), BF),
                pltpu.SemaphoreType.DMA((3,)),
            ],
        ),
        compiler_params=params(),
        cost_estimate=pl.CostEstimate(
            flops=COST * 20 * t * d * d, bytes_accessed=COST * (16 * t * d + 6 * d * d), transcendentals=0
        ),
        name="attention_inputs",
    )(sc, x, vec, vec, w, w_other, vec, cos, sin, om, idc)


def own_half_kernel(fq, fk, vals, idc, idr, num, den):
    t = fq.shape[1]
    same = idc[...] == idr[...]
    zero = jnp.zeros((t, LANES), BF)
    q, k = fq[0], fk[0]
    for p in range(GROUP // 2):
        v = vals[:, p * LANES : (p + 1) * LANES]
        total = None
        for e in range(2):
            fh = jnp.where(lane_is((t, GF), FEATS, 2 * p + e), q, zero)
            s = jnp.where(same, dot_t(fh, k), 0.0).astype(BF)
            mine = lane_is((t, LANES), HEAD, e)
            va = jnp.concatenate(
                [jnp.where(mine, v, zero), jnp.where(mine, jnp.ones_like(v), zero)], axis=1
            )
            more = dot(s, va)
            total = more if total is None else total + more
        num[:, p * LANES : (p + 1) * LANES] = total[:, :LANES]
        den[:, p * LANES : (p + 1) * LANES] = total[:, LANES:]


def own_half(f, vals, ids):
    idc, idr = ids
    t, d = vals.shape
    c2 = lambda g: (0, 0)
    col = lambda g: (0, g)
    return pl.pallas_call(
        own_half_kernel,
        grid=(HEADS // GROUP,),
        out_shape=[jax.ShapeDtypeStruct((t, d), F32)] * 2,
        in_specs=[
            pl.BlockSpec((1, t, GF), lambda g: (0, 0, g)),
            pl.BlockSpec((1, t, GF), lambda g: (1, 0, g)),
            pl.BlockSpec((t, GV), col),
            pl.BlockSpec((t, 1), c2),
            pl.BlockSpec((1, t), c2),
        ],
        out_specs=[pl.BlockSpec((t, GV), col)] * 2,
        compiler_params=params(),
        cost_estimate=pl.CostEstimate(flops=COST * (16 * t * t * d), bytes_accessed=COST * (12 * t * d), transcendentals=0),
        name="own_half",
    )(f, f, vals, idc, idr)


def outputs_kernel(
    sc, num, den, f, x, st, idc, bo, g2, b2, bu, bd, wo, wu, wd, wo_r, wu_r, wd_r,
    att, rden, mid, n2, act, gp, res, acc, ups, ups_too, wos, wus, wds, sems, *, layer,
):
    j = pl.program_id(0)
    steps = wus.shape[0]
    t, d = x.shape[1:]
    full = (slice(None), slice(None))
    up_at = lambda c: (slice(None), pl.ds(c * FCHUNK, FCHUNK))
    down_at = lambda c: (pl.ds(c * FCHUNK, FCHUNK), slice(None))

    @pl.when(j == 0)
    def _():
        copies(wo, wo_r, sc[0] == layer, full, wos, sems.at[0])
        for c in range(steps):
            copies(wu, wu_r, sc[0] == layer, up_at(c), wus.at[c], sems.at[1 + c])
            copies(wd, wd_r, sc[0] == layer, down_at(c), wds.at[c], sems.at[1 + steps + c])
        cross = crossing(sc, idc[...]).astype(BF)
        for g in range(HEADS // GROUP):
            cols = slice(g * GV, (g + 1) * GV)
            fqc = f[0, :, g * GF : (g + 1) * GF] * cross
            n = num[:, cols] + dot(fqc, widen_state(st[:, cols]))
            m = den[:, cols] + dot(fqc, widen_state(st[:, d + g * GV : d + (g + 1) * GV]))
            rd = 1.0 / m
            rden[:, cols] = rd
            att[:, cols] = (n * rd).astype(BF)
        arrived(wo, full, wos, sems.at[0])
        m = x[0].astype(F32) + dot(att[...], wos[...]) + bo[...]
        mid[...] = m
        xhat, _ = norm_parts(m)
        n2[...] = (xhat * g2[...] + b2[...]).astype(BF)
        acc[...] = m + bd[...]

    for c in range(steps):

        @pl.when(j == c)
        def _():
            arrived(wu, up_at(c), wus.at[c], sems.at[1 + c])

        @pl.when(j == c + 1)
        def _():
            arrived(wd, down_at(c), wds.at[c], sems.at[1 + steps + c])

    def product(into):
        into[...] = dot(n2[...], wus[jnp.minimum(j, steps - 1)]) + bu[...]

    def rest(ref):
        up = ref[...]
        phi, ex = gelu_parts(up)
        a = (up * phi).astype(BF)
        act[0] = a
        gp[...] = (phi + up * ex * (1.0 / math.sqrt(2.0 * math.pi))).astype(BF)
        acc[...] += dot(a, wds[jnp.maximum(j - 1, 0)])

    @pl.when(j == 0)
    def _():
        product(ups)

    @pl.when((j > 0) & (j < steps) & (j % 2 == 1))
    def _():
        product(ups_too)
        rest(ups)

    @pl.when((j > 0) & (j < steps) & (j % 2 == 0))
    def _():
        product(ups)
        rest(ups_too)

    @pl.when(j == steps)
    def _():
        rest(ups if steps % 2 == 1 else ups_too)
        res[...] = acc[...].astype(BF)


def forward_outputs(layer, sc, num, den, f, x, st, idc, vec, wts, which):
    wo, wu, wd = wts[:3]
    t, d = x.shape[1:]
    ff = wu.shape[1]
    steps = ff // FCHUNK
    c2 = lambda j, s: (0, 0)
    col = lambda j, s: (0, jnp.maximum(j - 1, 0))
    half_at = lambda j, s: (jnp.maximum(j - 1, 0) // (steps // 2), 0, jnp.maximum(j - 1, 0) % (steps // 2))
    ahead = BU * UNIT // FCHUNK
    return pl.pallas_call(
        partial(outputs_kernel, layer=layer),
        out_shape=[
            jax.ShapeDtypeStruct((t, d), BF),
            jax.ShapeDtypeStruct((t, d), F32),
            jax.ShapeDtypeStruct((t, d), F32),
            jax.ShapeDtypeStruct((t, d), BF),
            jax.ShapeDtypeStruct((2, t, ff // 2), BF),
            jax.ShapeDtypeStruct((t, ff), BF),
            jax.ShapeDtypeStruct((t, d), BF),
        ],
        grid_spec=pltpu.PrefetchScalarGridSpec(
            num_scalar_prefetch=1,
            grid=(steps + 1,),
            in_specs=[
                pl.BlockSpec((t, d), c2),
                pl.BlockSpec((t, d), c2),
                pl.BlockSpec((1, t, HEADS * FEATS), lambda j, s: (0, 0, 0)),
                pl.BlockSpec((1, t, d), which),
                pl.BlockSpec((FEATS, 2 * d), c2),
                pl.BlockSpec((t, 1), c2),
                vec_at(BO),
                vec_at(G2),
                vec_at(B2),
                pl.BlockSpec((1, FCHUNK), lambda j, s: (0, ahead + jnp.minimum(j, steps - 1))),
                vec_at(BD),
            ]
            + [ANY] * 6,
            out_specs=[
                pl.BlockSpec((t, d), c2),
                pl.BlockSpec((t, d), c2),
                pl.BlockSpec((t, d), c2),
                pl.BlockSpec((t, d), c2),
                pl.BlockSpec((1, t, FCHUNK), half_at),
                pl.BlockSpec((t, FCHUNK), col),
                pl.BlockSpec((t, d), c2),
            ],
            scratch_shapes=[
                pltpu.VMEM((t, d), F32),
                pltpu.VMEM((t, FCHUNK), F32),
                pltpu.VMEM((t, FCHUNK), F32),
                pltpu.VMEM((d, d), BF),
                pltpu.VMEM((steps, d, FCHUNK), BF),
                pltpu.VMEM((steps, FCHUNK, d), BF),
                pltpu.SemaphoreType.DMA((1 + 2 * steps,)),
            ],
        ),
        compiler_params=params(),
        cost_estimate=pl.CostEstimate(
            flops=COST * (4 * t * d * ff + 2 * t * d * d), bytes_accessed=COST * (4 * d * ff + 40 * t * d), transcendentals=0
        ),
        name="attention_out_and_ffn",
    )(sc, num, den, f, x, st, idc, vec, vec, vec, vec, vec, *wts)


def ffn_back_kernel(
    sc, g, gp, mid, g2, att, rden, f, idc, wd, wu, wo, wd_r, wu_r, wo_r,
    d_up, d_mid, d_br, d_num, d_den, dst, s_bd, s_bu, s_g2, s_b2, s_bo,
    acc, wos, wus, wds, sems, *, layer,
):
    j = pl.program_id(0)
    steps = wus.shape[0]
    t, d = g.shape[1:]
    full = (slice(None), slice(None))
    up_at = lambda c: (slice(None), pl.ds(c * FCHUNK, FCHUNK))
    down_at = lambda c: (pl.ds(c * FCHUNK, FCHUNK), slice(None))

    @pl.when(j == 0)
    def _():
        for c in range(steps):
            copies(wd, wd_r, sc[0] == layer, down_at(c), wds.at[c], sems.at[1 + steps + c])
            copies(wu, wu_r, sc[0] == layer, up_at(c), wus.at[c], sems.at[1 + c])
        copies(wo, wo_r, sc[0] == layer, full, wos, sems.at[0])
        acc[...] = jnp.zeros_like(acc)
        s_bd[...] = jnp.sum(g[0].astype(F32), axis=0, keepdims=True)

    for c in range(steps):

        @pl.when(j == c)
        def _():
            arrived(wu, up_at(c), wus.at[c], sems.at[1 + c])
            arrived(wd, down_at(c), wds.at[c], sems.at[1 + steps + c])

    d_act = dot_t(g[0], wds[j])
    up = (d_act * gp[...].astype(F32)).astype(BF)
    d_up[...] = up
    s_bu[...] = jnp.sum(up.astype(F32), axis=0, keepdims=True)
    acc[...] += dot_t(up, wus[j])

    @pl.when(j == pl.num_programs(0) - 1)
    def _():
        arrived(wo, full, wos, sems.at[0])
        shape = (GV, GV)
        ones = (
            lax.broadcasted_iota(jnp.int32, shape, 0) // HEAD
            == lax.broadcasted_iota(jnp.int32, shape, 1) // HEAD
        ).astype(BF)
        dn2 = acc[...]
        xhat, r = norm_parts(mid[...])
        dm = g[0].astype(F32) + norm_back(dn2, xhat, r, g2[...])
        s_g2[...] = jnp.sum(dn2 * xhat, axis=0, keepdims=True)
        s_b2[...] = jnp.sum(dn2, axis=0, keepdims=True)
        d_mid[...] = dm
        db = dm.astype(BF)
        d_br[...] = db
        s_bo[...] = jnp.sum(db.astype(F32), axis=0, keepdims=True)
        cr = crossing(sc, idc[...]).astype(BF)
        for k in range(HEADS // GROUP):
            cols = slice(k * GV, (k + 1) * GV)
            da = dot_t(db, wos[cols, :]) * rden[:, cols]
            dnb = da.astype(BF)
            d_num[:, cols] = dnb
            hi, lo = split(da * att[:, cols].astype(F32))
            ddb = (-(dot(hi, ones) + dot(lo, ones))).astype(BF)
            d_den[:, cols] = ddb
            fq = f[0, :, k * GF : (k + 1) * GF] * cr
            dst[:, cols] = squeeze_state(tdot(fq, dnb)).astype(BF)
            dst[:, d + k * GV : d + (k + 1) * GV] = squeeze_state(tdot(fq, ddb)).astype(BF)


def ffn_back(layer, sc, g, gp, mid, vec, att, rden, f, idc, wts, which):
    wu = wts[1]
    t, d = g.shape[1:]
    ff = wu.shape[1]
    steps = ff // FCHUNK
    c2 = lambda j, s: (0, 0)
    col = lambda j, s: (0, j)
    line_shape = jax.ShapeDtypeStruct((1, d), F32)
    wide = jax.ShapeDtypeStruct((t, d), BF)
    tile = pl.BlockSpec((t, d), c2)
    line = pl.BlockSpec((1, d), c2)
    return pl.pallas_call(
        partial(ffn_back_kernel, layer=layer),
        out_shape=[
            jax.ShapeDtypeStruct((t, ff), BF),
            jax.ShapeDtypeStruct((t, d), F32),
            wide,
            wide,
            wide,
            jax.ShapeDtypeStruct((FEATS, 2 * d), BF),
            line_shape,
            jax.ShapeDtypeStruct((1, ff), F32),
            line_shape,
            line_shape,
            line_shape,
        ],
        grid_spec=pltpu.PrefetchScalarGridSpec(
            num_scalar_prefetch=1,
            grid=(steps,),
            in_specs=[
                pl.BlockSpec((1, t, d), which),
                pl.BlockSpec((t, FCHUNK), col),
                tile,
                vec_at(G2),
                tile,
                tile,
                pl.BlockSpec((1, t, HEADS * FEATS), lambda j, s: (0, 0, 0)),
                pl.BlockSpec((t, 1), c2),
            ]
            + [ANY] * 6,
            out_specs=[
                pl.BlockSpec((t, FCHUNK), col),
                tile,
                tile,
                tile,
                tile,
                pl.BlockSpec((FEATS, 2 * d), c2),
                line,
                pl.BlockSpec((1, FCHUNK), col),
                line,
                line,
                line,
            ],
            scratch_shapes=[
                pltpu.VMEM((t, d), F32),
                pltpu.VMEM((d, d), BF),
                pltpu.VMEM((steps, d, FCHUNK), BF),
                pltpu.VMEM((steps, FCHUNK, d), BF),
                pltpu.SemaphoreType.DMA((1 + 2 * steps,)),
            ],
        ),
        compiler_params=params(),
        cost_estimate=pl.CostEstimate(
            flops=COST * (4 * t * d * ff + 4 * t * d * d), bytes_accessed=COST * (4 * d * ff + 40 * t * d), transcendentals=0
        ),
        name="ffn_back",
    )(sc, g, gp, mid, vec, att, rden, f, idc, *wts)


def attention_back_kernel(
    sc, f, vals, d_num, d_den, u, st, dst, idc, idr, cos, sin, om, *rest, layer
):
    t, d = vals.shape
    both_parts = len(rest) > 2
    if both_parts:
        x, gain, d_mid, w, w_other, d_proj, s_bq, d_in, s_g1, s_b1, ws, sems = rest
        fetch_weights(sc[0] == layer, w, w_other, ws, sems)
    else:
        d_proj, s_bq = rest
    hi, lo = split(expanded(om[...]))
    ones = expanded(jnp.ones((HEAD, GF), F32)).astype(BF)
    cross = crossing(sc, idc[...])
    same = idc[...] == idr[...]
    cr = cross.astype(BF)
    head_lane = lax.broadcasted_iota(jnp.int32, (t, GV), 1) % HEAD == 0
    one_lane = jnp.where(head_lane, cross, 0.0).astype(BF)

    hi_hi = jnp.concatenate([hi, hi], axis=1)
    one_one = jnp.concatenate([ones, ones], axis=1)

    for k in range(HEADS // GROUP):
        cols = slice(k * GV, (k + 1) * GV)
        tail = slice(d + k * GV, d + (k + 1) * GV)
        fcols = slice(k * GF, (k + 1) * GF)
        fq, fk = f[0, :, fcols], f[1, :, fcols]
        zf = jnp.zeros_like(fq)
        vg, dn, dd = vals[:, cols], d_num[:, cols], d_den[:, cols]
        dd1 = jnp.where(head_lane, dd, jnp.zeros_like(dd))
        state, tots = widen_state(st[:, cols]), widen_state(st[:, tail])
        d_state, d_tots = widen_state(dst[:, cols]), widen_state(dst[:, tail])
        dfq = dot_t(dn * cr, state) + dot_t(dd1 * cr, tots)
        dfk = dot_t(vg * cr, d_state) + dot_t(one_lane, d_tots)
        dv = dot(fk * cr, d_state)
        dvs = []
        for p in range(GROUP // 2):
            own = slice(p * LANES, (p + 1) * LANES)
            v1 = jnp.concatenate([vg[:, own], jnp.ones((t, LANES), BF)], axis=1)
            dvp = dv[:, own]
            for e in range(2):
                feat_lane = lane_is((t, GF), FEATS, 2 * p + e)
                mine = lane_is((t, LANES), HEAD, e)
                zero = jnp.zeros((t, LANES), BF)
                fqh, fkh = jnp.where(feat_lane, fq, zf), jnp.where(feat_lane, fk, zf)
                dnh = jnp.where(mine, dn[:, own], zero)
                ah = jnp.concatenate([dnh, jnp.where(mine, dd1[:, own], zero)], axis=1)
                pt = jnp.where(same, dot_t(ah, v1), 0.0).astype(BF)
                dfq = dfq + dot(pt, fkh)
                dfk = dfk + tdot(pt, fqh)
                pt = jnp.where(same, dot_t(fkh, fq), 0.0).astype(BF)
                dvp = dvp + dot(pt, dnh)
            dvs.append(dvp)
        parts = [jnp.concatenate(dvs, axis=1).astype(BF)]
        for q, (df, ft) in enumerate(((dfq, fq), (dfk, fk))):
            dz = df * ft.astype(F32)
            zh, zl = split(dz)
            both = jnp.concatenate([zh, zl], axis=1)
            du = dot_t(both, hi_hi) + dot_t(zh, lo) - u[q, :, cols] * dot_t(both, one_one)
            for e in range(2):
                a = du[:, e * LANES : (e + 1) * LANES]
                parts.append((a * cos[...] - half_turn(a) * sin[...]).astype(BF))
        for at, part in ((2 * d, parts[0]), (0, jnp.concatenate(parts[1:3], axis=1)), (d, jnp.concatenate(parts[3:], axis=1))):
            here = slice(at + k * GV, at + (k + 1) * GV)
            d_proj[:, here] = part
            s_bq[:, here] = jnp.sum(part.astype(F32), axis=0, keepdims=True)

    if both_parts:
        finish_inputs(d_proj, x, gain, d_mid, w, d_in, s_g1, s_b1, ws, sems)


def third(i, d):
    return (slice(None), pl.ds(i * d, d))


def fetch_weights(mine, w, w_other, ws, sems):
    for i in range(3):
        copies(w, w_other, mine, third(i, ws.shape[1]), ws.at[i], sems.at[i])


def finish_inputs(d_proj, x, gain, d_mid, w, d_in, s_g1, s_b1, ws, sems):
    d = ws.shape[1]
    dn1 = None
    for i in range(3):
        arrived(w, third(i, d), ws.at[i], sems.at[i])
        part = dot_t(d_proj[:, i * d : (i + 1) * d], ws[i])
        dn1 = part if dn1 is None else dn1 + part
    xhat, r = norm_parts(x[0].astype(F32))
    d_in[...] = (d_mid[...] + norm_back(dn1, xhat, r, gain[...])).astype(BF)
    s_g1[...] = jnp.sum(dn1 * xhat, axis=0, keepdims=True)
    s_b1[...] = jnp.sum(dn1, axis=0, keepdims=True)


def inputs_back_kernel(sc, d_proj, x, gain, d_mid, w, w_other, d_in, s_g1, s_b1, ws, sems, *, layer):
    fetch_weights(sc[0] == layer, w, w_other, ws, sems)
    finish_inputs(d_proj, x, gain, d_mid, w, d_in, s_g1, s_b1, ws, sems)


def whole(a):
    return pl.BlockSpec(a.shape, lambda j, s: (0,) * len(a.shape))


def input_specs(d_mid, which):
    t, d = d_mid.shape
    shapes = [
        jax.ShapeDtypeStruct((t, d), BF),
        jax.ShapeDtypeStruct((1, d), F32),
        jax.ShapeDtypeStruct((1, d), F32),
    ]
    specs = [pl.BlockSpec((1, t, d), which), vec_at(G1), whole(d_mid), ANY, ANY]
    return shapes, specs, [pltpu.VMEM((3, d, d), BF), pltpu.SemaphoreType.DMA((3,))]


def attention_back(layer, sc, f, vals, d_num, d_den, u, st, dst, ids, tables, om, inputs):
    t, d = vals.shape
    operands = [f, vals, d_num, d_den, u, st, dst, *ids, *tables, om]
    specs = [whole(a) for a in operands]
    shapes = [jax.ShapeDtypeStruct((t, 3 * d), BF), jax.ShapeDtypeStruct((1, 3 * d), F32)]
    scratch = []
    if inputs is not None:
        x, vec, d_mid, w, w_other, which = inputs
        more, more_specs, scratch = input_specs(d_mid, which)
        operands += [x, vec, d_mid, w, w_other]
        specs += more_specs
        shapes += more
    return pl.pallas_call(
        partial(attention_back_kernel, layer=layer),
        out_shape=shapes,
        grid_spec=pltpu.PrefetchScalarGridSpec(
            num_scalar_prefetch=1,
            grid=(1,),
            in_specs=specs,
            out_specs=[whole(a) for a in shapes],
            scratch_shapes=scratch,
        ),
        compiler_params=params(),
        cost_estimate=pl.CostEstimate(
            flops=COST * 48 * t * t * d, bytes_accessed=COST * 40 * t * d, transcendentals=0
        ),
        name="attention_back",
    )(sc, *operands)


def inputs_back(layer, sc, d_proj, x, vec, d_mid, w, w_other, which):
    t, d = d_mid.shape
    shapes, specs, scratch = input_specs(d_mid, which)
    return pl.pallas_call(
        partial(inputs_back_kernel, layer=layer),
        out_shape=shapes,
        grid_spec=pltpu.PrefetchScalarGridSpec(
            num_scalar_prefetch=1,
            grid=(1,),
            in_specs=[whole(d_proj)] + specs,
            out_specs=[whole(a) for a in shapes],
            scratch_shapes=scratch,
        ),
        compiler_params=params(),
        cost_estimate=pl.CostEstimate(
            flops=COST * 6 * t * d * d, bytes_accessed=COST * 16 * t * d, transcendentals=0
        ),
        name="inputs_back",
    )(sc, d_proj, x, vec, d_mid, w, w_other)


ROWS = UNIT // 2


def weight_grad_kernel(sc, *refs, sizes, dims):
    send, keep = refs[-2:]
    at = 0
    for m, size in enumerate(sizes):
        left, left_r, right, right_r = refs[4 * m : 4 * m + 4]

        @pl.when((pl.program_id(0) >= at) & (pl.program_id(0) < at + size))
        def _():
            total = tdot(left[0], right[0]) + tdot(left_r[0], right_r[0])
            low, high = total[:, :ROWS].astype(BF), total[:, ROWS:].astype(BF)

            @pl.when(bit_of(sc, dims) == 0)
            def _():
                keep[0] = low
                send[0] = high

            @pl.when(bit_of(sc, dims) == 1)
            def _():
                keep[0] = high
                send[0] = low

        at += size


def weight_grad(sc, members, dims):
    sizes = [m[-1] for m in members]
    operands, specs, at = [], [], 0
    for left, lp, left_r, lrp, right, rp, right_r, rrp, size in members:
        t = left.shape[1]
        here = lambda i, at=at, size=size: jnp.clip(i - at, 0, size - 1)
        operands += [left, left_r, right, right_r]
        specs += [
            pl.BlockSpec((1, t, ROWS), lambda i, s, f=lp, h=here: f(h(i), s[0])),
            pl.BlockSpec((1, t, ROWS), lambda i, s, f=lrp, h=here: f(h(i), s[0])),
            pl.BlockSpec((1, t, UNIT), lambda i, s, f=rp, h=here: f(h(i), s[0])),
            pl.BlockSpec((1, t, UNIT), lambda i, s, f=rrp, h=here: f(h(i), s[0])),
        ]
        at += size
    shape = jax.ShapeDtypeStruct((at, ROWS, ROWS), BF)
    spec = pl.BlockSpec((1, ROWS, ROWS), lambda i, s: (i, 0, 0))
    return pl.pallas_call(
        partial(weight_grad_kernel, sizes=sizes, dims=dims),
        out_shape=[shape, shape],
        grid_spec=pltpu.PrefetchScalarGridSpec(
            num_scalar_prefetch=1, grid=(at,), in_specs=specs, out_specs=[spec, spec]
        ),
        compiler_params=params(),
        cost_estimate=pl.CostEstimate(
            flops=COST * 2 * at * t * UNIT * UNIT, bytes_accessed=COST * at * 4 * t * UNIT, transcendentals=0
        ),
        name="weight_grad",
    )(sc, *operands)


def chip_bits():
    wide, row = lax.axis_index("wide"), lax.axis_index("row")
    return {"x": wide % 2, "y": row, "z0": wide // 2 % 2, "z1": wide // 4}


def bit_of(sc, dims):
    if dims is None:
        return 0
    at = [1 + ("x", "y", "z0", "z1").index(d) for d in dims]
    return jnp.where(sc[0] == 0, sc[at[0]], sc[at[1]])


class Links:
    def __init__(self):
        self.section = lax.axis_index("section")
        self.bits = chip_bits()

    def bit(self, dims):
        return jnp.where(self.section == 0, self.bits[dims[0]], self.bits[dims[1]])

    def swap(self, value, dims):
        flips = {"x": (0, 1), "y": (1, 0), "z0": (0, 2), "z1": (0, 4)}
        pairs = []
        for s in range(2):
            fr, fw = flips[dims[s]]
            for r in range(2):
                for w in range(8):
                    pairs.append(((s * 2 + r) * 8 + w, (s * 2 + (r ^ fr)) * 8 + (w ^ fw)))
        return lax.ppermute(value, ("section", "row", "wide"), pairs)


AXES = {"x": "x", "y": "y", "z": "z0", "w": "z1"}


def pick(parts, bit):
    total = None
    for p in parts:
        one = lax.dynamic_index_in_dim(p, bit, 0, keepdims=False).astype(F32)
        total = one if total is None else total + one
    return total.astype(BF)


def add(parts):
    return parts[0] + parts[1]


def join(own, other, bit):
    return jnp.stack([jnp.where(bit == 0, own, other), jnp.where(bit == 0, other, own)])


def fence_kernel(token, out):
    pass


def fence(token, values):
    (token,) = after([token], values)
    return pl.pallas_call(
        fence_kernel,
        out_shape=jax.ShapeDtypeStruct(token.shape, token.dtype),
        in_specs=[pl.BlockSpec(memory_space=pl.ANY)],
        out_specs=pl.BlockSpec(memory_space=pl.ANY),
        input_output_aliases={0: 0},
        compiler_params=params(1),
        cost_estimate=pl.CostEstimate(flops=10**12, bytes_accessed=10**9, transcendentals=0),
        name="fence",
    )(token)


def scattered_sum(value):
    part = lax.psum_scatter(value, ("row", "wide"), scatter_dimension=0, tiled=True)
    return lax.all_gather(part, ("row", "wide"), axis=0, tiled=True)


def after(values, others):
    values, others = list(values), list(others)
    if not others:
        return values
    return list(lax.optimization_barrier(tuple(values + others)))[: len(values)]


SWAP = [(0, 1), (1, 0)]


class Flow:
    def __init__(self, links, kinds, owner):
        self.links, self.owner = links, owner
        self.step = 0
        self.order = None if links is None else [tuple(AXES[a] for a in dims) for dims in zip(*kinds)]

    def first_dims(self):
        return None if self.links is None else self.order[0]

    def begin(self, send, keep):
        self.shape = send.shape
        self.parts = keep
        if self.links is None:
            self.flight = send
        else:
            self.flight = self.links.swap(send, self.order[0])

    def advance(self, others=()):
        (came,) = after([self.flight], others)
        self.step += 1
        step = self.step
        if self.links is None:
            return self.plain(came)
        if step == 6:
            self.flight = self.over(came)
            self.mine = (self.parts, came)
            return [came]
        if step == 7:
            (early,) = after([self.early], others)
            self.result = (*self.mine, early, came)
            return [came, early]
        if step == 1:
            shape = (2, self.shape[0] * self.shape[1] // 2, self.shape[2])
            self.parts = [self.parts.reshape(shape), came.reshape(shape)]
            dims = self.order[1]
            send = pick(self.parts, 1 - self.links.bit(dims))
        elif step == 2:
            dims = self.order[2]
            send = self.parts = add([pick(self.parts, self.links.bit(self.order[1])), came])
        elif step == 3:
            dims = self.order[3]
            send = self.parts = add([self.parts, came])
        elif step == 4:
            dims = self.order[1]
            send = self.parts = add([self.parts, came])
        else:
            dims = self.order[0]
            send = self.parts = join(self.parts, came, self.links.bit(self.order[1])).reshape(self.shape)
        self.flight = self.links.swap(send, dims)
        if step == 5:
            self.early = self.over(send)
        return [send]

    def over(self, value):
        return lax.ppermute(value, "section", SWAP)

    def plain(self, came):
        total = jnp.concatenate([self.parts, came], axis=0)
        mine = scattered_sum(total.reshape(-1, ROWS)).reshape((2,) + self.shape)
        self.result = (mine[0], mine[1], self.over(mine[0]), self.over(mine[1]))
        return []


def finish_kernel(sc, *refs, dims):
    out = refs[-1]
    for layer in range(2):
        for side in range(2):
            half = layer if side == 0 else 1 - layer
            ends = dims[layer] if side == 0 or dims[layer] is None else dims[layer][::-1]
            for bit in range(2):
                here = (sc[0] == layer) & (bit_of(sc, ends) == bit)

                @pl.when(here)
                def _():
                    at = 4 * layer + 2 * side
                    out[half, :, :ROWS] = refs[at + bit][0].astype(F32)
                    out[half, :, ROWS:] = refs[at + 1 - bit][0].astype(F32)


def finish(sc, first, second, start, units, by_row, dims):
    spec = lambda layer: pl.BlockSpec(
        (1, ROWS, ROWS), lambda u, s: (start + jnp.where(s[0] == layer, u, 0), 0, 0)
    )
    if by_row:
        shape, place = (2, units * ROWS, UNIT), lambda u, s: (0, u, 0)
    else:
        shape, place = (2, ROWS, units * UNIT), lambda u, s: (0, 0, u)
    out = pl.pallas_call(
        partial(finish_kernel, dims=dims),
        out_shape=jax.ShapeDtypeStruct(shape, F32),
        grid_spec=pltpu.PrefetchScalarGridSpec(
            num_scalar_prefetch=1,
            grid=(units,),
            in_specs=[spec(0)] * 4 + [spec(1)] * 4,
            out_specs=pl.BlockSpec((2, ROWS, UNIT), place),
        ),
        compiler_params=params(),
        cost_estimate=pl.CostEstimate(
            flops=COST * units * UNIT * UNIT, bytes_accessed=COST * units * 8 * UNIT * UNIT, transcendentals=0
        ),
        name="finish",
    )(sc, *first, *second)
    return out.reshape(1, -1, shape[2])


def local(
    inputs, cotangent, segment_ids, step_number, redraw_every, bank_offset,
    ln1_gain, ln1_bias, w_qkv, b_qkv, w_out, b_out, ln2_gain, ln2_bias,
    w_up, b_up, w_down, b_down, bank,
):
    section = lax.axis_index("section")
    row = lax.axis_index("row")
    first = section == 0
    t, d = inputs.shape[1:]
    ff = w_up.shape[2]
    swap = [(0, 1), (1, 0)]

    def both(own):
        other = lax.ppermute(own, "section", swap)
        return own, other

    w_qkv, w_qkv_r = both(w_qkv[0])
    chosen = (bank_offset[0] + step_number[0] // redraw_every[0]) % bank.shape[1]
    omega = lax.dynamic_index_in_dim(bank[0], chosen, 0, keepdims=False)
    vectors = pack([ln1_gain, ln1_bias, b_qkv, b_out, ln2_gain, ln2_bias, b_up, b_down])
    vectors_r = lax.ppermute(vectors, "section", swap)
    omega, omega_r = both(jnp.concatenate([omega] * GROUP, axis=1))
    w_out, w_out_r = both(w_out[0])
    w_up, w_up_r = both(w_up[0])
    w_down, w_down_r = both(w_down[0])

    lane = lax.broadcasted_iota(jnp.int32, (t, LANES), 1) % HEAD
    place = (row * t + lax.broadcasted_iota(jnp.int32, (t, LANES), 0)).astype(F32)
    angles = place * (10000.0 ** (-2.0 * (lane % (HEAD // 2)).astype(F32) / HEAD))
    scale = HEAD ** (-0.25)
    tables = (jnp.cos(angles) * scale, jnp.sin(angles) * jnp.where(lane < HEAD // 2, -scale, scale))

    own_ids = lax.dynamic_slice(segment_ids, (section, row * t), (1, t))
    edge = lax.dynamic_slice(segment_ids, (section, jnp.int32(t - 1)), (1, 2))[0]
    ids = (own_ids.reshape(t, 1), own_ids)
    other_row = [(i, i ^ 1) for i in range(2)]
    by_section = lambda j, s: (s[0], 0, 0)
    only = lambda j, s: (0, 0, 0)

    sc = jnp.concatenate([jnp.stack([section, *chip_bits().values()]), edge]).astype(jnp.int32)
    saved, given = [], []
    x, which = inputs, by_section
    for layer in range(2):
        mine = section == layer
        vec = jnp.where(mine, vectors, vectors_r)
        om = jnp.where(mine, omega, omega_r)
        normed, u, f, vals, st = forward_inputs(layer, sc, x, vec, w_qkv, w_qkv_r, tables, om, ids[0], which)
        st = lax.ppermute(st, "row", other_row)
        num, den = own_half(f, vals, ids)
        att, rden, mid, n2, act, gp, res = forward_outputs(
            layer, sc, num, den, f, x, st, ids[0], vec, (w_out, w_up, w_down, w_out_r, w_up_r, w_down_r), which
        )
        saved.append((sc, x, vec, om, which, normed, u, f, vals, st, att, rden, mid, n2, act, gp))
        x, which = res[None], only
        given.append([lax.ppermute(g, "section", swap) for g in (n2, att, normed, act)])
    outs = (saved[1][1][0], x[0])

    def to_owner(of_layer):
        mine = jnp.where(first, of_layer[0], of_layer[1])
        other = lax.ppermute(jnp.where(first, of_layer[1], of_layer[0]), "section", swap)
        return join(mine, other, section)[None]

    hidden = to_owner(outs)

    links = Links() if lax.axis_size("wide") == 8 else None
    flows = {
        name + str(layer): Flow(links, KINDS[name + str(layer)], layer)
        for layer in range(2)
        for name in "duq"
    }
    at_own = lambda i, s: (s, 0, 0)
    at_other = lambda i, s: (1 - s, 0, 0)
    at_first = lambda i, s: (0, 0, 0)
    at_unit = lambda i, s: (0, 0, i)
    grads = {1: (cotangent, at_own, cotangent, at_other)}
    parts, back, done = {}, {}, {}
    shown = []

    def tied(value):
        (value,) = after([value], shown)
        shown.clear()
        return value

    def members(name):
        layer = int(name[1])
        normed, att, n2, act = (saved[layer][i] for i in (5, 10, 13, 14))
        gave_n2, gave_att, gave_normed, gave_act = given[layer]
        if name[0] == "d":
            left = (act, lambda i, s: (s, 0, i), gave_act, lambda i, s: (s, 0, i))
            return [(*left, *grads[layer], ff // UNIT)]

        def one(own, other, right, units):
            return (
                own[None], lambda i, s: (0, 0, s), other[None], lambda i, s: (0, 0, s),
                right[0][None], at_unit, right[1][None], at_unit, units,
            )

        if name[0] == "u":
            return [
                one(n2, gave_n2, done["up", layer], ff // UNIT),
                one(att, gave_att, done["br", layer], 1),
            ]
        return [one(normed, gave_normed, done["proj", layer], 3)]

    def run(item):
        name, layer = item[:2], int(item[1])
        if name in flows and len(item) == 2:
            before = list(shown)
            shown.clear()
            shown.extend(flows[name].advance(before))
        elif name in flows:
            send, keep = weight_grad(tied(sc), members(name), flows[name].first_dims())
            shown.append(send)
            flows[name].begin(send, keep)
        elif name[0] == "f":
            _, x, vec, om, which, normed, u, f, vals, st, att, rden, mid, n2, act, gp = saved[layer]
            g = grads[layer][0]
            back[layer] = ffn_back(
                layer, sc, g, tied(gp), mid, vec, att, rden, f, ids[0],
                (w_down, w_up, w_out, w_down_r, w_up_r, w_out_r),
                by_section if layer == 1 else only,
            )
            shown.append(back[layer][0])
            done["dst", layer] = lax.ppermute(back[layer][5], "row", other_row)
            done["up", layer] = both(back[layer][0])
            done["br", layer] = both(back[layer][2])
        elif name[0] == "a":
            _, x, vec, om, which, normed, u, f, vals, st = saved[layer][:10]
            d_mid, _, d_num, d_den = back[layer][1:5]
            out = attention_back(
                layer, sc, f, vals, tied(d_num), d_den, u, st, done["dst", layer], ids, tables, om,
                (x, vec, d_mid, w_qkv, w_qkv_r, which) if layer == 1 else None,
            )
            shown.append(out[0])
            done["proj", layer] = both(out[0])
            parts[layer] = out[1]
            if layer == 1:
                done["in", 1] = out[2:]
                own, other = both(out[2])
                grads[0] = (own[None], at_first, other[None], at_first)
        elif name[0] == "i":
            _, x, vec, om, which = saved[layer][:5]
            done["in", 0] = inputs_back(
                layer, sc, tied(done["proj", 0][0]), x, vec, back[0][1], w_qkv, w_qkv_r, which
            )
            shown.append(done["in", 0][0])
        elif name[0] == "s":
            smalls = []
            for k in range(2):
                s_bd, s_bu, s_g2, s_b2, s_bo = back[k][6:]
                smalls += [*done["in", k][1:], parts[k], s_bo, s_g2, s_b2, s_bu, s_bd]
            done["small"] = lax.psum(tied(pack(smalls)), ("section", "row", "wide"))
        else:
            kind, start, units, by_row = MATRICES[name]
            firsts, seconds = flows[kind + "0"].result, flows[kind + "1"].result
            dims = [flows[kind + str(k)].first_dims() for k in range(2)]
            done[name] = finish(tied(sc), firsts, seconds, start, units, by_row, dims)
            shown.append(done[name])

    token, fenced = jnp.zeros((8, LANES), F32), False
    for item in ORDER if links is not None else PLAIN:
        run(item)
        fenced = fenced or item == LAST
        if fenced and links is not None:
            token = fence(token, shown)
            shown[:] = [token]
    both_layers = done["small"].reshape(2, -1) + token[:1, :1]
    small = lax.dynamic_slice_in_dim(both_layers, section, 1)
    input_grads = to_owner((done["in", 0][0], done["in", 1][0]))
    g1, b1, bq, bo, gain2, bias2, bu, bd = cut(small, d, ff)
    return (
        hidden, input_grads, g1, b1, done["m0"], bq, done["m1"], bo,
        gain2, bias2, done["m2"], bu, done["m3"], bd,
    )


MATRICES = {"m0": ("q", 0, 3, False), "m1": ("u", 4, 1, False), "m2": ("u", 0, 4, False), "m3": ("d", 0, 4, True)}

KINDS = {
    "d1": ("yxwz", "xyzw"),
    "u1": ("xzwy", "zywx"),
    "q1": ("wyxz", "yxzw"),
    "d0": ("yxzw", "xywz"),
    "u0": ("xyzw", "yxwz"),
    "q0": ("yxwz", "xyzw"),
}

ORDER = (
    "f1", "d1w", "a1", "d1", "u1w", "d1", "d0w", "f0", "d0", "d1", "q1w", "d0", "a0", "u1", "u0w", "d0", "u1",
    "q0w", "q1", "u0", "i0", "d1", "q0", "q1", "u0", "d0", "s0", "d1", "q1", "d0", "u0", "u1", "d1", "q0",
    "q1", "d0", "u1", "u0", "q0", "u1", "q1", "u0", "q0", "d1", "d0", "m3", "q0", "u1", "u0", "q1", "u1",
    "u0", "m1", "q1", "q0", "m2", "q0", "m0",
)

LAST = "i0"

PLAIN = (
    "d1w", "d1", "f1", "u1w", "u1", "a1", "q1w", "q1", "d0w", "d0", "f0", "u0w", "u0", "a0", "q0w", "q0",
    "i0", "s0", "m3", "m2", "m1", "m0",
)


def cut(vec, d, ff):
    out, at = [], 0
    for size in (d, d, 3 * d, d, d, d, ff, d):
        out.append(vec[:, at : at + size])
        at += size
    return out


def solution(mesh):
    return jax.shard_map(
        local,
        mesh=mesh,
        in_specs=(
            P("wide", "row", None),
            P("wide", "row", None),
            P("wide", None),
            P(),
            P(),
            P(),
            P("section", None),
            P("section", None),
            P("section", None, None),
            P("section", None),
            P("section", None, None),
            P("section", None),
            P("section", None),
            P("section", None),
            P("section", None, None),
            P("section", None),
            P("section", None, None),
            P("section", None),
            P("section", None, None, None),
        ),
        out_specs=(
            P("section", "wide", "row", None),
            P("section", "wide", "row", None),
            P("section", None),
            P("section", None),
            P("section", None, None),
            P("section", None),
            P("section", None, None),
            P("section", None),
            P("section", None),
            P("section", None),
            P("section", None, None),
            P("section", None),
            P("section", None, None),
            P("section", None),
        ),
        check_vma=False,
    )
```

```python
from functools import partial
import math

import jax
import jax.numpy as jnp
from jax import lax
from jax.experimental import pallas as pl
from jax.experimental.pallas import tpu as pltpu
from jax.sharding import PartitionSpec as P

HEADS = 12
HEAD = 64
FEATS = 32
EPS = 1e-05
F32 = jnp.float32
BF = jnp.bfloat16
LANES = 128
GROUP = 4
GV = GROUP * HEAD
GF = GROUP * FEATS
FCHUNK = 768
COST = 30


def dot(a, b, dims=((1,), (0,))):
    return lax.dot_general(a, b, (dims, ((), ())), preferred_element_type=F32)


def dot_t(a, b):
    return dot(a, b, ((1,), (1,)))


def tdot(a, b):
    return dot(a, b, ((0,), (0,)))


def expanded(om):
    shape = (GV, GF)
    same = (
        lax.broadcasted_iota(jnp.int32, shape, 0) // HEAD
        == lax.broadcasted_iota(jnp.int32, shape, 1) // FEATS
    )
    return jnp.where(same, jnp.concatenate([om] * GROUP, axis=0), 0.0)


def crossing(sc, ids):
    return jnp.where((ids == sc[5]) & (sc[5] == sc[6]), 1.0, 0.0)


def split(v):
    high = v.astype(BF)
    return high, (v - high.astype(F32)).astype(BF)


def norm_parts(v):
    c = v - jnp.mean(v, axis=-1, keepdims=True)
    r = lax.rsqrt(jnp.mean(c * c, axis=-1, keepdims=True) + EPS)
    return c * r, r


def norm_back(d, xhat, r, gain):
    e = d * gain
    m1 = jnp.mean(e, axis=-1, keepdims=True)
    m2 = jnp.mean(e * xhat, axis=-1, keepdims=True)
    return (e - m1 - xhat * m2) * r


def gelu_parts(x):
    z = jnp.abs(x) * (1.0 / math.sqrt(2.0))
    ex = jnp.exp(-z * z)
    t = pl.reciprocal(1.0 + 0.3275911 * z, approx=True)
    p = 0.5 * 1.061405429
    for c in (-1.453152027, 1.421413741, -0.284496736, 0.254829592):
        p = p * t + 0.5 * c
    q = p * t * ex
    return jnp.where(x < 0, q, 1.0 - q), ex


def lane_is(shape, width, k):
    return lax.broadcasted_iota(jnp.int32, shape, 1) // width == k


def half_turn(a):
    low = lax.broadcasted_iota(jnp.int32, a.shape, 1) % HEAD < HEAD // 2
    return jnp.where(low, pltpu.roll(a, 96, 1), pltpu.roll(a, 32, 1))


def block_mask(dtype):
    shape = (GF, GV)
    same = (
        lax.broadcasted_iota(jnp.int32, shape, 0) // FEATS
        == lax.broadcasted_iota(jnp.int32, shape, 1) // HEAD
    )
    return same.astype(dtype)


def squeeze_state(st):
    st = st * block_mask(F32)
    return st[0:32] + st[32:64] + st[64:96] + st[96:128]


def widen_state(st):
    return jnp.concatenate([st] * GROUP, axis=0) * block_mask(st.dtype)


def pack_kernel(*refs):
    out, at = refs[-1], 0
    for ref in refs[:-1]:
        width = ref.shape[1]
        out[:, at : at + width] = ref[...]
        at += width


def pack(arrays):
    width = sum(a.shape[1] for a in arrays)
    return pl.pallas_call(
        pack_kernel,
        grid=(1,),
        in_specs=[pl.BlockSpec(a.shape, lambda i: (0, 0)) for a in arrays],
        out_specs=pl.BlockSpec((1, width), lambda i: (0, 0)),
        out_shape=jax.ShapeDtypeStruct((1, width), F32),
        compiler_params=params(),
        cost_estimate=pl.CostEstimate(flops=10**10, bytes_accessed=10**8, transcendentals=0),
        name="pack",
    )(*arrays)


def copies(own, other, mine, at, dst, sem):
    @pl.when(mine)
    def _():
        pltpu.make_async_copy(own.at[at], dst, sem).start()

    @pl.when(jnp.logical_not(mine))
    def _():
        pltpu.make_async_copy(other.at[at], dst, sem).start()


def arrived(own, at, dst, sem):
    pltpu.make_async_copy(own.at[at], dst, sem).wait()


ANY = pl.BlockSpec(memory_space=pl.ANY)


def params(mib=60):
    return pltpu.CompilerParams(vmem_limit_bytes=mib * 1024 * 1024)


def inputs_kernel(
    sc, x, gain, bias, w, w_other, bq, cos, sin, om, idc,
    normed, u, f, vals, st, ws, oma, sqm, sems, *, layer,
):
    j = pl.program_id(0)
    d = x.shape[2]
    at = lambda i: (slice(None), pl.ds(i * d, d))

    @pl.when(j == 0)
    def _():
        for i in range(3):
            copies(w, w_other, sc[0] == layer, at(i), ws.at[i], sems.at[i])
        xhat, _ = norm_parts(x[0].astype(F32))
        normed[...] = (xhat * gain[...] + bias[...]).astype(BF)
        hi, lo = split(expanded(om[...]))
        oma[:, :GF] = hi
        oma[:, GF:] = lo
        sqm[...] = expanded(jnp.full((HEAD, GF), -0.5, F32)).astype(BF)

    for i in range(3):

        @pl.when(j == i)
        def _():
            arrived(w, at(i), ws.at[i], sems.at[i])

    @pl.when(j < 2)
    def _():
        for g in range(HEADS // GROUP):
            cols = slice(g * GV, (g + 1) * GV)
            pr = dot(normed[...], ws[j, :, cols]) + bq[:, cols]
            parts = []
            for e in range(2):
                a = pr[:, e * LANES : (e + 1) * LANES]
                parts.append(a * cos[...] + half_turn(a) * sin[...])
            turned = jnp.concatenate(parts, axis=1)
            u[0, :, cols] = turned
            uh, ul = split(turned)
            sh, sl = split(turned * turned)
            ex = dot(uh, oma[...])
            ex = ex[:, :GF] + ex[:, GF:] + dot(ul, oma[:, :GF])
            ex = ex + dot(sh, sqm[...]) + dot(sl, sqm[...])
            f[0, :, g * GF : (g + 1) * GF] = (jnp.exp(ex) * (1.0 / math.sqrt(FEATS))).astype(BF)

    @pl.when(j == 2)
    def _():
        cross = crossing(sc, idc[...]).astype(BF)
        for g in range(HEADS // GROUP):
            cols = slice(g * GV, (g + 1) * GV)
            v = (dot(normed[...], ws[2, :, cols]) + bq[:, cols]).astype(BF)
            vals[:, cols] = v
            fk = f[0, :, g * GF : (g + 1) * GF] * cross
            one = jnp.ones_like(v)
            st[:, cols] = squeeze_state(tdot(fk, v)).astype(BF)
            st[:, d + g * GV : d + (g + 1) * GV] = squeeze_state(tdot(fk, one)).astype(BF)


UNIT = 768
G1, B1, BQ, BO, G2, B2, BU, BD = 0, 1, 2, 5, 6, 7, 8, 12


def vec_at(block):
    return pl.BlockSpec((1, UNIT), lambda j, s: (0, block))


def forward_inputs(layer, sc, x, vec, w, w_other, tables, om, idc, which):
    cos, sin = tables
    t, d = x.shape[1:]
    fw = HEADS * FEATS
    c2 = lambda j, s: (0, 0)
    part = lambda j, s: (jnp.minimum(j, 1), 0, 0)
    return pl.pallas_call(
        partial(inputs_kernel, layer=layer),
        out_shape=[
            jax.ShapeDtypeStruct((t, d), BF),
            jax.ShapeDtypeStruct((2, t, d), F32),
            jax.ShapeDtypeStruct((2, t, fw), BF),
            jax.ShapeDtypeStruct((t, d), BF),
            jax.ShapeDtypeStruct((FEATS, 2 * d), BF),
        ],
        grid_spec=pltpu.PrefetchScalarGridSpec(
            num_scalar_prefetch=1,
            grid=(3,),
            in_specs=[
                pl.BlockSpec((1, t, d), which),
                vec_at(G1),
                vec_at(B1),
                ANY,
                ANY,
                pl.BlockSpec((1, UNIT), lambda j, s: (0, BQ + j)),
                pl.BlockSpec((t, LANES), c2),
                pl.BlockSpec((t, LANES), c2),
                pl.BlockSpec((HEAD, GF), c2),
                pl.BlockSpec((t, 1), c2),
            ],
            out_specs=[
                pl.BlockSpec((t, d), c2),
                pl.BlockSpec((1, t, d), part),
                pl.BlockSpec((1, t, fw), part),
                pl.BlockSpec((t, d), c2),
                pl.BlockSpec((FEATS, 2 * d), c2),
            ],
            scratch_shapes=[
                pltpu.VMEM((3, d, d), BF),
                pltpu.VMEM((GV, GV), BF),
                pltpu.VMEM((GV, GF), BF),
                pltpu.SemaphoreType.DMA((3,)),
            ],
        ),
        compiler_params=params(),
        cost_estimate=pl.CostEstimate(
            flops=COST * 20 * t * d * d, bytes_accessed=COST * (16 * t * d + 6 * d * d), transcendentals=0
        ),
        name="attention_inputs",
    )(sc, x, vec, vec, w, w_other, vec, cos, sin, om, idc)


def own_half_kernel(fq, fk, vals, idc, idr, num, den):
    t = fq.shape[1]
    same = idc[...] == idr[...]
    zero = jnp.zeros((t, LANES), BF)
    q, k = fq[0], fk[0]
    for p in range(GROUP // 2):
        v = vals[:, p * LANES : (p + 1) * LANES]
        total = None
        for e in range(2):
            fh = jnp.where(lane_is((t, GF), FEATS, 2 * p + e), q, zero)
            s = jnp.where(same, dot_t(fh, k), 0.0).astype(BF)
            mine = lane_is((t, LANES), HEAD, e)
            va = jnp.concatenate(
                [jnp.where(mine, v, zero), jnp.where(mine, jnp.ones_like(v), zero)], axis=1
            )
            more = dot(s, va)
            total = more if total is None else total + more
        num[:, p * LANES : (p + 1) * LANES] = total[:, :LANES]
        den[:, p * LANES : (p + 1) * LANES] = total[:, LANES:]


def own_half(f, vals, ids):
    idc, idr = ids
    t, d = vals.shape
    c2 = lambda g: (0, 0)
    col = lambda g: (0, g)
    return pl.pallas_call(
        own_half_kernel,
        grid=(HEADS // GROUP,),
        out_shape=[jax.ShapeDtypeStruct((t, d), F32)] * 2,
        in_specs=[
            pl.BlockSpec((1, t, GF), lambda g: (0, 0, g)),
            pl.BlockSpec((1, t, GF), lambda g: (1, 0, g)),
            pl.BlockSpec((t, GV), col),
            pl.BlockSpec((t, 1), c2),
            pl.BlockSpec((1, t), c2),
        ],
        out_specs=[pl.BlockSpec((t, GV), col)] * 2,
        compiler_params=params(),
        cost_estimate=pl.CostEstimate(flops=COST * (16 * t * t * d), bytes_accessed=COST * (12 * t * d), transcendentals=0),
        name="own_half",
    )(f, f, vals, idc, idr)


def outputs_kernel(
    sc, num, den, f, x, st, idc, bo, g2, b2, bu, bd, wo, wu, wd, wo_r, wu_r, wd_r,
    att, rden, mid, n2, act, gp, res, acc, ups, ups_too, wos, wus, wds, sems, *, layer,
):
    j = pl.program_id(0)
    steps = wus.shape[0]
    t, d = x.shape[1:]
    full = (slice(None), slice(None))
    up_at = lambda c: (slice(None), pl.ds(c * FCHUNK, FCHUNK))
    down_at = lambda c: (pl.ds(c * FCHUNK, FCHUNK), slice(None))

    @pl.when(j == 0)
    def _():
        copies(wo, wo_r, sc[0] == layer, full, wos, sems.at[0])
        for c in range(steps):
            copies(wu, wu_r, sc[0] == layer, up_at(c), wus.at[c], sems.at[1 + c])
            copies(wd, wd_r, sc[0] == layer, down_at(c), wds.at[c], sems.at[1 + steps + c])
        cross = crossing(sc, idc[...]).astype(BF)
        for g in range(HEADS // GROUP):
            cols = slice(g * GV, (g + 1) * GV)
            fqc = f[0, :, g * GF : (g + 1) * GF] * cross
            n = num[:, cols] + dot(fqc, widen_state(st[:, cols]))
            m = den[:, cols] + dot(fqc, widen_state(st[:, d + g * GV : d + (g + 1) * GV]))
            rd = 1.0 / m
            rden[:, cols] = rd
            att[:, cols] = (n * rd).astype(BF)
        arrived(wo, full, wos, sems.at[0])
        m = x[0].astype(F32) + dot(att[...], wos[...]) + bo[...]
        mid[...] = m
        xhat, _ = norm_parts(m)
        n2[...] = (xhat * g2[...] + b2[...]).astype(BF)
        acc[...] = m + bd[...]

    for c in range(steps):

        @pl.when(j == c)
        def _():
            arrived(wu, up_at(c), wus.at[c], sems.at[1 + c])

        @pl.when(j == c + 1)
        def _():
            arrived(wd, down_at(c), wds.at[c], sems.at[1 + steps + c])

    def product(into):
        into[...] = dot(n2[...], wus[jnp.minimum(j, steps - 1)]) + bu[...]

    def rest(ref):
        up = ref[...]
        phi, ex = gelu_parts(up)
        a = (up * phi).astype(BF)
        act[0] = a
        gp[...] = (phi + up * ex * (1.0 / math.sqrt(2.0 * math.pi))).astype(BF)
        acc[...] += dot(a, wds[jnp.maximum(j - 1, 0)])

    @pl.when(j == 0)
    def _():
        product(ups)

    @pl.when((j > 0) & (j < steps) & (j % 2 == 1))
    def _():
        product(ups_too)
        rest(ups)

    @pl.when((j > 0) & (j < steps) & (j % 2 == 0))
    def _():
        product(ups)
        rest(ups_too)

    @pl.when(j == steps)
    def _():
        rest(ups if steps % 2 == 1 else ups_too)
        res[...] = acc[...].astype(BF)


def forward_outputs(layer, sc, num, den, f, x, st, idc, vec, wts, which):
    wo, wu, wd = wts[:3]
    t, d = x.shape[1:]
    ff = wu.shape[1]
    steps = ff // FCHUNK
    c2 = lambda j, s: (0, 0)
    col = lambda j, s: (0, jnp.maximum(j - 1, 0))
    half_at = lambda j, s: (jnp.maximum(j - 1, 0) // (steps // 2), 0, jnp.maximum(j - 1, 0) % (steps // 2))
    ahead = BU * UNIT // FCHUNK
    return pl.pallas_call(
        partial(outputs_kernel, layer=layer),
        out_shape=[
            jax.ShapeDtypeStruct((t, d), BF),
            jax.ShapeDtypeStruct((t, d), F32),
            jax.ShapeDtypeStruct((t, d), F32),
            jax.ShapeDtypeStruct((t, d), BF),
            jax.ShapeDtypeStruct((2, t, ff // 2), BF),
            jax.ShapeDtypeStruct((t, ff), BF),
            jax.ShapeDtypeStruct((t, d), BF),
        ],
        grid_spec=pltpu.PrefetchScalarGridSpec(
            num_scalar_prefetch=1,
            grid=(steps + 1,),
            in_specs=[
                pl.BlockSpec((t, d), c2),
                pl.BlockSpec((t, d), c2),
                pl.BlockSpec((1, t, HEADS * FEATS), lambda j, s: (0, 0, 0)),
                pl.BlockSpec((1, t, d), which),
                pl.BlockSpec((FEATS, 2 * d), c2),
                pl.BlockSpec((t, 1), c2),
                vec_at(BO),
                vec_at(G2),
                vec_at(B2),
                pl.BlockSpec((1, FCHUNK), lambda j, s: (0, ahead + jnp.minimum(j, steps - 1))),
                vec_at(BD),
            ]
            + [ANY] * 6,
            out_specs=[
                pl.BlockSpec((t, d), c2),
                pl.BlockSpec((t, d), c2),
                pl.BlockSpec((t, d), c2),
                pl.BlockSpec((t, d), c2),
                pl.BlockSpec((1, t, FCHUNK), half_at),
                pl.BlockSpec((t, FCHUNK), col),
                pl.BlockSpec((t, d), c2),
            ],
            scratch_shapes=[
                pltpu.VMEM((t, d), F32),
                pltpu.VMEM((t, FCHUNK), F32),
                pltpu.VMEM((t, FCHUNK), F32),
                pltpu.VMEM((d, d), BF),
                pltpu.VMEM((steps, d, FCHUNK), BF),
                pltpu.VMEM((steps, FCHUNK, d), BF),
                pltpu.SemaphoreType.DMA((1 + 2 * steps,)),
            ],
        ),
        compiler_params=params(),
        cost_estimate=pl.CostEstimate(
            flops=COST * (4 * t * d * ff + 2 * t * d * d), bytes_accessed=COST * (4 * d * ff + 40 * t * d), transcendentals=0
        ),
        name="attention_out_and_ffn",
    )(sc, num, den, f, x, st, idc, vec, vec, vec, vec, vec, *wts)


def ffn_back_kernel(
    sc, g, gp, mid, g2, att, rden, f, idc, wd, wu, wo, wd_r, wu_r, wo_r,
    d_up, d_mid, d_br, d_num, d_den, dst, s_bd, s_bu, s_g2, s_b2, s_bo,
    acc, wos, wus, wds, sems, *, layer,
):
    j = pl.program_id(0)
    steps = wus.shape[0]
    t, d = g.shape[1:]
    full = (slice(None), slice(None))
    up_at = lambda c: (slice(None), pl.ds(c * FCHUNK, FCHUNK))
    down_at = lambda c: (pl.ds(c * FCHUNK, FCHUNK), slice(None))

    @pl.when(j == 0)
    def _():
        for c in range(steps):
            copies(wd, wd_r, sc[0] == layer, down_at(c), wds.at[c], sems.at[1 + steps + c])
            copies(wu, wu_r, sc[0] == layer, up_at(c), wus.at[c], sems.at[1 + c])
        copies(wo, wo_r, sc[0] == layer, full, wos, sems.at[0])
        acc[...] = jnp.zeros_like(acc)
        s_bd[...] = jnp.sum(g[0].astype(F32), axis=0, keepdims=True)

    for c in range(steps):

        @pl.when(j == c)
        def _():
            arrived(wu, up_at(c), wus.at[c], sems.at[1 + c])
            arrived(wd, down_at(c), wds.at[c], sems.at[1 + steps + c])

    d_act = dot_t(g[0], wds[j])
    up = (d_act * gp[...].astype(F32)).astype(BF)
    d_up[...] = up
    s_bu[...] = jnp.sum(up.astype(F32), axis=0, keepdims=True)
    acc[...] += dot_t(up, wus[j])

    @pl.when(j == pl.num_programs(0) - 1)
    def _():
        arrived(wo, full, wos, sems.at[0])
        shape = (GV, GV)
        ones = (
            lax.broadcasted_iota(jnp.int32, shape, 0) // HEAD
            == lax.broadcasted_iota(jnp.int32, shape, 1) // HEAD
        ).astype(BF)
        dn2 = acc[...]
        xhat, r = norm_parts(mid[...])
        dm = g[0].astype(F32) + norm_back(dn2, xhat, r, g2[...])
        s_g2[...] = jnp.sum(dn2 * xhat, axis=0, keepdims=True)
        s_b2[...] = jnp.sum(dn2, axis=0, keepdims=True)
        d_mid[...] = dm
        db = dm.astype(BF)
        d_br[...] = db
        s_bo[...] = jnp.sum(db.astype(F32), axis=0, keepdims=True)
        cr = crossing(sc, idc[...]).astype(BF)
        for k in range(HEADS // GROUP):
            cols = slice(k * GV, (k + 1) * GV)
            da = dot_t(db, wos[cols, :]) * rden[:, cols]
            dnb = da.astype(BF)
            d_num[:, cols] = dnb
            hi, lo = split(da * att[:, cols].astype(F32))
            ddb = (-(dot(hi, ones) + dot(lo, ones))).astype(BF)
            d_den[:, cols] = ddb
            fq = f[0, :, k * GF : (k + 1) * GF] * cr
            dst[:, cols] = squeeze_state(tdot(fq, dnb)).astype(BF)
            dst[:, d + k * GV : d + (k + 1) * GV] = squeeze_state(tdot(fq, ddb)).astype(BF)


def ffn_back(layer, sc, g, gp, mid, vec, att, rden, f, idc, wts, which):
    wu = wts[1]
    t, d = g.shape[1:]
    ff = wu.shape[1]
    steps = ff // FCHUNK
    c2 = lambda j, s: (0, 0)
    col = lambda j, s: (0, j)
    line_shape = jax.ShapeDtypeStruct((1, d), F32)
    wide = jax.ShapeDtypeStruct((t, d), BF)
    tile = pl.BlockSpec((t, d), c2)
    line = pl.BlockSpec((1, d), c2)
    return pl.pallas_call(
        partial(ffn_back_kernel, layer=layer),
        out_shape=[
            jax.ShapeDtypeStruct((t, ff), BF),
            jax.ShapeDtypeStruct((t, d), F32),
            wide,
            wide,
            wide,
            jax.ShapeDtypeStruct((FEATS, 2 * d), BF),
            line_shape,
            jax.ShapeDtypeStruct((1, ff), F32),
            line_shape,
            line_shape,
            line_shape,
        ],
        grid_spec=pltpu.PrefetchScalarGridSpec(
            num_scalar_prefetch=1,
            grid=(steps,),
            in_specs=[
                pl.BlockSpec((1, t, d), which),
                pl.BlockSpec((t, FCHUNK), col),
                tile,
                vec_at(G2),
                tile,
                tile,
                pl.BlockSpec((1, t, HEADS * FEATS), lambda j, s: (0, 0, 0)),
                pl.BlockSpec((t, 1), c2),
            ]
            + [ANY] * 6,
            out_specs=[
                pl.BlockSpec((t, FCHUNK), col),
                tile,
                tile,
                tile,
                tile,
                pl.BlockSpec((FEATS, 2 * d), c2),
                line,
                pl.BlockSpec((1, FCHUNK), col),
                line,
                line,
                line,
            ],
            scratch_shapes=[
                pltpu.VMEM((t, d), F32),
                pltpu.VMEM((d, d), BF),
                pltpu.VMEM((steps, d, FCHUNK), BF),
                pltpu.VMEM((steps, FCHUNK, d), BF),
                pltpu.SemaphoreType.DMA((1 + 2 * steps,)),
            ],
        ),
        compiler_params=params(),
        cost_estimate=pl.CostEstimate(
            flops=COST * (4 * t * d * ff + 4 * t * d * d), bytes_accessed=COST * (4 * d * ff + 40 * t * d), transcendentals=0
        ),
        name="ffn_back",
    )(sc, g, gp, mid, vec, att, rden, f, idc, *wts)


def attention_back_kernel(
    sc, f, vals, d_num, d_den, u, st, dst, idc, idr, cos, sin, om, *rest, layer
):
    t, d = vals.shape
    both_parts = len(rest) > 2
    if both_parts:
        x, gain, d_mid, w, w_other, d_proj, s_bq, d_in, s_g1, s_b1, ws, sems = rest
        fetch_weights(sc[0] == layer, w, w_other, ws, sems)
    else:
        d_proj, s_bq = rest
    hi, lo = split(expanded(om[...]))
    ones = expanded(jnp.ones((HEAD, GF), F32)).astype(BF)
    cross = crossing(sc, idc[...])
    same = idc[...] == idr[...]
    cr = cross.astype(BF)
    head_lane = lax.broadcasted_iota(jnp.int32, (t, GV), 1) % HEAD == 0
    one_lane = jnp.where(head_lane, cross, 0.0).astype(BF)

    hi_hi = jnp.concatenate([hi, hi], axis=1)
    one_one = jnp.concatenate([ones, ones], axis=1)

    for k in range(HEADS // GROUP):
        cols = slice(k * GV, (k + 1) * GV)
        tail = slice(d + k * GV, d + (k + 1) * GV)
        fcols = slice(k * GF, (k + 1) * GF)
        fq, fk = f[0, :, fcols], f[1, :, fcols]
        zf = jnp.zeros_like(fq)
        vg, dn, dd = vals[:, cols], d_num[:, cols], d_den[:, cols]
        dd1 = jnp.where(head_lane, dd, jnp.zeros_like(dd))
        state, tots = widen_state(st[:, cols]), widen_state(st[:, tail])
        d_state, d_tots = widen_state(dst[:, cols]), widen_state(dst[:, tail])
        dfq = dot_t(dn * cr, state) + dot_t(dd1 * cr, tots)
        dfk = dot_t(vg * cr, d_state) + dot_t(one_lane, d_tots)
        dv = dot(fk * cr, d_state)
        dvs = []
        for p in range(GROUP // 2):
            own = slice(p * LANES, (p + 1) * LANES)
            v1 = jnp.concatenate([vg[:, own], jnp.ones((t, LANES), BF)], axis=1)
            dvp = dv[:, own]
            for e in range(2):
                feat_lane = lane_is((t, GF), FEATS, 2 * p + e)
                mine = lane_is((t, LANES), HEAD, e)
                zero = jnp.zeros((t, LANES), BF)
                fqh, fkh = jnp.where(feat_lane, fq, zf), jnp.where(feat_lane, fk, zf)
                dnh = jnp.where(mine, dn[:, own], zero)
                ah = jnp.concatenate([dnh, jnp.where(mine, dd1[:, own], zero)], axis=1)
                pt = jnp.where(same, dot_t(ah, v1), 0.0).astype(BF)
                dfq = dfq + dot(pt, fkh)
                dfk = dfk + tdot(pt, fqh)
                pt = jnp.where(same, dot_t(fkh, fq), 0.0).astype(BF)
                dvp = dvp + dot(pt, dnh)
            dvs.append(dvp)
        parts = [jnp.concatenate(dvs, axis=1).astype(BF)]
        for q, (df, ft) in enumerate(((dfq, fq), (dfk, fk))):
            dz = df * ft.astype(F32)
            zh, zl = split(dz)
            both = jnp.concatenate([zh, zl], axis=1)
            du = dot_t(both, hi_hi) + dot_t(zh, lo) - u[q, :, cols] * dot_t(both, one_one)
            for e in range(2):
                a = du[:, e * LANES : (e + 1) * LANES]
                parts.append((a * cos[...] - half_turn(a) * sin[...]).astype(BF))
        for at, part in ((2 * d, parts[0]), (0, jnp.concatenate(parts[1:3], axis=1)), (d, jnp.concatenate(parts[3:], axis=1))):
            here = slice(at + k * GV, at + (k + 1) * GV)
            d_proj[:, here] = part
            s_bq[:, here] = jnp.sum(part.astype(F32), axis=0, keepdims=True)

    if both_parts:
        finish_inputs(d_proj, x, gain, d_mid, w, d_in, s_g1, s_b1, ws, sems)


def third(i, d):
    return (slice(None), pl.ds(i * d, d))


def fetch_weights(mine, w, w_other, ws, sems):
    for i in range(3):
        copies(w, w_other, mine, third(i, ws.shape[1]), ws.at[i], sems.at[i])


def finish_inputs(d_proj, x, gain, d_mid, w, d_in, s_g1, s_b1, ws, sems):
    d = ws.shape[1]
    dn1 = None
    for i in range(3):
        arrived(w, third(i, d), ws.at[i], sems.at[i])
        part = dot_t(d_proj[:, i * d : (i + 1) * d], ws[i])
        dn1 = part if dn1 is None else dn1 + part
    xhat, r = norm_parts(x[0].astype(F32))
    d_in[...] = (d_mid[...] + norm_back(dn1, xhat, r, gain[...])).astype(BF)
    s_g1[...] = jnp.sum(dn1 * xhat, axis=0, keepdims=True)
    s_b1[...] = jnp.sum(dn1, axis=0, keepdims=True)


def inputs_back_kernel(sc, d_proj, x, gain, d_mid, w, w_other, d_in, s_g1, s_b1, ws, sems, *, layer):
    fetch_weights(sc[0] == layer, w, w_other, ws, sems)
    finish_inputs(d_proj, x, gain, d_mid, w, d_in, s_g1, s_b1, ws, sems)


def whole(a):
    return pl.BlockSpec(a.shape, lambda j, s: (0,) * len(a.shape))


def input_specs(d_mid, which):
    t, d = d_mid.shape
    shapes = [
        jax.ShapeDtypeStruct((t, d), BF),
        jax.ShapeDtypeStruct((1, d), F32),
        jax.ShapeDtypeStruct((1, d), F32),
    ]
    specs = [pl.BlockSpec((1, t, d), which), vec_at(G1), whole(d_mid), ANY, ANY]
    return shapes, specs, [pltpu.VMEM((3, d, d), BF), pltpu.SemaphoreType.DMA((3,))]


def attention_back(layer, sc, f, vals, d_num, d_den, u, st, dst, ids, tables, om, inputs):
    t, d = vals.shape
    operands = [f, vals, d_num, d_den, u, st, dst, *ids, *tables, om]
    specs = [whole(a) for a in operands]
    shapes = [jax.ShapeDtypeStruct((t, 3 * d), BF), jax.ShapeDtypeStruct((1, 3 * d), F32)]
    scratch = []
    if inputs is not None:
        x, vec, d_mid, w, w_other, which = inputs
        more, more_specs, scratch = input_specs(d_mid, which)
        operands += [x, vec, d_mid, w, w_other]
        specs += more_specs
        shapes += more
    return pl.pallas_call(
        partial(attention_back_kernel, layer=layer),
        out_shape=shapes,
        grid_spec=pltpu.PrefetchScalarGridSpec(
            num_scalar_prefetch=1,
            grid=(1,),
            in_specs=specs,
            out_specs=[whole(a) for a in shapes],
            scratch_shapes=scratch,
        ),
        compiler_params=params(),
        cost_estimate=pl.CostEstimate(
            flops=COST * 48 * t * t * d, bytes_accessed=COST * 40 * t * d, transcendentals=0
        ),
        name="attention_back",
    )(sc, *operands)


def inputs_back(layer, sc, d_proj, x, vec, d_mid, w, w_other, which):
    t, d = d_mid.shape
    shapes, specs, scratch = input_specs(d_mid, which)
    return pl.pallas_call(
        partial(inputs_back_kernel, layer=layer),
        out_shape=shapes,
        grid_spec=pltpu.PrefetchScalarGridSpec(
            num_scalar_prefetch=1,
            grid=(1,),
            in_specs=[whole(d_proj)] + specs,
            out_specs=[whole(a) for a in shapes],
            scratch_shapes=scratch,
        ),
        compiler_params=params(),
        cost_estimate=pl.CostEstimate(
            flops=COST * 6 * t * d * d, bytes_accessed=COST * 16 * t * d, transcendentals=0
        ),
        name="inputs_back",
    )(sc, d_proj, x, vec, d_mid, w, w_other)


ROWS = UNIT // 2


def weight_grad_kernel(sc, *refs, sizes, dims):
    send, keep = refs[-2:]
    at = 0
    for m, size in enumerate(sizes):
        left, left_r, right, right_r = refs[4 * m : 4 * m + 4]

        @pl.when((pl.program_id(0) >= at) & (pl.program_id(0) < at + size))
        def _():
            total = tdot(left[0], right[0]) + tdot(left_r[0], right_r[0])
            low, high = total[:, :ROWS].astype(BF), total[:, ROWS:].astype(BF)

            @pl.when(bit_of(sc, dims) == 0)
            def _():
                keep[0] = low
                send[0] = high

            @pl.when(bit_of(sc, dims) == 1)
            def _():
                keep[0] = high
                send[0] = low

        at += size


def weight_grad(sc, members, dims):
    sizes = [m[-1] for m in members]
    operands, specs, at = [], [], 0
    for left, lp, left_r, lrp, right, rp, right_r, rrp, size in members:
        t = left.shape[1]
        here = lambda i, at=at, size=size: jnp.clip(i - at, 0, size - 1)
        operands += [left, left_r, right, right_r]
        specs += [
            pl.BlockSpec((1, t, ROWS), lambda i, s, f=lp, h=here: f(h(i), s[0])),
            pl.BlockSpec((1, t, ROWS), lambda i, s, f=lrp, h=here: f(h(i), s[0])),
            pl.BlockSpec((1, t, UNIT), lambda i, s, f=rp, h=here: f(h(i), s[0])),
            pl.BlockSpec((1, t, UNIT), lambda i, s, f=rrp, h=here: f(h(i), s[0])),
        ]
        at += size
    shape = jax.ShapeDtypeStruct((at, ROWS, ROWS), BF)
    spec = pl.BlockSpec((1, ROWS, ROWS), lambda i, s: (i, 0, 0))
    return pl.pallas_call(
        partial(weight_grad_kernel, sizes=sizes, dims=dims),
        out_shape=[shape, shape],
        grid_spec=pltpu.PrefetchScalarGridSpec(
            num_scalar_prefetch=1, grid=(at,), in_specs=specs, out_specs=[spec, spec]
        ),
        compiler_params=params(),
        cost_estimate=pl.CostEstimate(
            flops=COST * 2 * at * t * UNIT * UNIT, bytes_accessed=COST * at * 4 * t * UNIT, transcendentals=0
        ),
        name="weight_grad",
    )(sc, *operands)


def chip_bits():
    wide, row = lax.axis_index("wide"), lax.axis_index("row")
    return {"x": wide % 2, "y": row, "z0": wide // 2 % 2, "z1": wide // 4}


def bit_of(sc, dims):
    if dims is None:
        return 0
    at = [1 + ("x", "y", "z0", "z1").index(d) for d in dims]
    return jnp.where(sc[0] == 0, sc[at[0]], sc[at[1]])


class Links:
    def __init__(self):
        self.section = lax.axis_index("section")
        self.bits = chip_bits()

    def bit(self, dims):
        return jnp.where(self.section == 0, self.bits[dims[0]], self.bits[dims[1]])

    def swap(self, value, dims):
        flips = {"x": (0, 1), "y": (1, 0), "z0": (0, 2), "z1": (0, 4)}
        pairs = []
        for s in range(2):
            fr, fw = flips[dims[s]]
            for r in range(2):
                for w in range(8):
                    pairs.append(((s * 2 + r) * 8 + w, (s * 2 + (r ^ fr)) * 8 + (w ^ fw)))
        return lax.ppermute(value, ("section", "row", "wide"), pairs)


AXES = {"x": "x", "y": "y", "z": "z0", "w": "z1"}


def pick(parts, bit):
    total = None
    for p in parts:
        one = lax.dynamic_index_in_dim(p, bit, 0, keepdims=False).astype(F32)
        total = one if total is None else total + one
    return total.astype(BF)


def add(parts):
    return parts[0] + parts[1]


def join(own, other, bit):
    return jnp.stack([jnp.where(bit == 0, own, other), jnp.where(bit == 0, other, own)])


def fence_kernel(token, out):
    pass


def fence(token, values):
    (token,) = after([token], values)
    return pl.pallas_call(
        fence_kernel,
        out_shape=jax.ShapeDtypeStruct(token.shape, token.dtype),
        in_specs=[pl.BlockSpec(memory_space=pl.ANY)],
        out_specs=pl.BlockSpec(memory_space=pl.ANY),
        input_output_aliases={0: 0},
        compiler_params=params(1),
        cost_estimate=pl.CostEstimate(flops=10**12, bytes_accessed=10**9, transcendentals=0),
        name="fence",
    )(token)


def scattered_sum(value):
    part = lax.psum_scatter(value, ("row", "wide"), scatter_dimension=0, tiled=True)
    return lax.all_gather(part, ("row", "wide"), axis=0, tiled=True)


def after(values, others):
    values, others = list(values), list(others)
    if not others:
        return values
    return list(lax.optimization_barrier(tuple(values + others)))[: len(values)]


SWAP = [(0, 1), (1, 0)]


class Flow:
    def __init__(self, links, kinds, owner):
        self.links, self.owner = links, owner
        self.step = 0
        self.order = None if links is None else [tuple(AXES[a] for a in dims) for dims in zip(*kinds)]

    def first_dims(self):
        return None if self.links is None else self.order[0]

    def begin(self, send, keep):
        self.shape = send.shape
        self.parts = keep
        if self.links is None:
            self.flight = send
        else:
            self.flight = self.links.swap(send, self.order[0])

    def advance(self, others=()):
        (came,) = after([self.flight], others)
        self.step += 1
        step = self.step
        if self.links is None:
            return self.plain(came)
        if step == 6:
            self.flight = self.over(came)
            self.mine = (self.parts, came)
            return [came]
        if step == 7:
            (early,) = after([self.early], others)
            self.result = (*self.mine, early, came)
            return [came, early]
        if step == 1:
            shape = (2, self.shape[0] * self.shape[1] // 2, self.shape[2])
            self.parts = [self.parts.reshape(shape), came.reshape(shape)]
            dims = self.order[1]
            send = pick(self.parts, 1 - self.links.bit(dims))
        elif step == 2:
            dims = self.order[2]
            send = self.parts = add([pick(self.parts, self.links.bit(self.order[1])), came])
        elif step == 3:
            dims = self.order[3]
            send = self.parts = add([self.parts, came])
        elif step == 4:
            dims = self.order[1]
            send = self.parts = add([self.parts, came])
        else:
            dims = self.order[0]
            send = self.parts = join(self.parts, came, self.links.bit(self.order[1])).reshape(self.shape)
        self.flight = self.links.swap(send, dims)
        if step == 5:
            self.early = self.over(send)
        return [send]

    def over(self, value):
        return lax.ppermute(value, "section", SWAP)

    def plain(self, came):
        total = jnp.concatenate([self.parts, came], axis=0)
        mine = scattered_sum(total.reshape(-1, ROWS)).reshape((2,) + self.shape)
        self.result = (mine[0], mine[1], self.over(mine[0]), self.over(mine[1]))
        return []


def finish_kernel(sc, *refs, dims):
    out = refs[-1]
    for layer in range(2):
        for side in range(2):
            half = layer if side == 0 else 1 - layer
            ends = dims[layer] if side == 0 or dims[layer] is None else dims[layer][::-1]
            for bit in range(2):
                here = (sc[0] == layer) & (bit_of(sc, ends) == bit)

                @pl.when(here)
                def _():
                    at = 4 * layer + 2 * side
                    out[half, :, :ROWS] = refs[at + bit][0].astype(F32)
                    out[half, :, ROWS:] = refs[at + 1 - bit][0].astype(F32)


def finish(sc, first, second, start, units, by_row, dims):
    spec = lambda layer: pl.BlockSpec(
        (1, ROWS, ROWS), lambda u, s: (start + jnp.where(s[0] == layer, u, 0), 0, 0)
    )
    if by_row:
        shape, place = (2, units * ROWS, UNIT), lambda u, s: (0, u, 0)
    else:
        shape, place = (2, ROWS, units * UNIT), lambda u, s: (0, 0, u)
    out = pl.pallas_call(
        partial(finish_kernel, dims=dims),
        out_shape=jax.ShapeDtypeStruct(shape, F32),
        grid_spec=pltpu.PrefetchScalarGridSpec(
            num_scalar_prefetch=1,
            grid=(units,),
            in_specs=[spec(0)] * 4 + [spec(1)] * 4,
            out_specs=pl.BlockSpec((2, ROWS, UNIT), place),
        ),
        compiler_params=params(),
        cost_estimate=pl.CostEstimate(
            flops=COST * units * UNIT * UNIT, bytes_accessed=COST * units * 8 * UNIT * UNIT, transcendentals=0
        ),
        name="finish",
    )(sc, *first, *second)
    return out.reshape(1, -1, shape[2])


def local(
    inputs, cotangent, segment_ids, step_number, redraw_every, bank_offset,
    ln1_gain, ln1_bias, w_qkv, b_qkv, w_out, b_out, ln2_gain, ln2_bias,
    w_up, b_up, w_down, b_down, bank,
):
    section = lax.axis_index("section")
    row = lax.axis_index("row")
    first = section == 0
    t, d = inputs.shape[1:]
    ff = w_up.shape[2]
    swap = [(0, 1), (1, 0)]

    def both(own):
        other = lax.ppermute(own, "section", swap)
        return own, other

    w_qkv, w_qkv_r = both(w_qkv[0])
    chosen = (bank_offset[0] + step_number[0] // redraw_every[0]) % bank.shape[1]
    omega = lax.dynamic_index_in_dim(bank[0], chosen, 0, keepdims=False)
    vectors = pack([ln1_gain, ln1_bias, b_qkv, b_out, ln2_gain, ln2_bias, b_up, b_down])
    vectors_r = lax.ppermute(vectors, "section", swap)
    omega, omega_r = both(jnp.concatenate([omega] * GROUP, axis=1))
    w_out, w_out_r = both(w_out[0])
    w_up, w_up_r = both(w_up[0])
    w_down, w_down_r = both(w_down[0])

    lane = lax.broadcasted_iota(jnp.int32, (t, LANES), 1) % HEAD
    place = (row * t + lax.broadcasted_iota(jnp.int32, (t, LANES), 0)).astype(F32)
    angles = place * (10000.0 ** (-2.0 * (lane % (HEAD // 2)).astype(F32) / HEAD))
    scale = HEAD ** (-0.25)
    tables = (jnp.cos(angles) * scale, jnp.sin(angles) * jnp.where(lane < HEAD // 2, -scale, scale))

    own_ids = lax.dynamic_slice(segment_ids, (section, row * t), (1, t))
    edge = lax.dynamic_slice(segment_ids, (section, jnp.int32(t - 1)), (1, 2))[0]
    ids = (own_ids.reshape(t, 1), own_ids)
    other_row = [(i, i ^ 1) for i in range(2)]
    by_section = lambda j, s: (s[0], 0, 0)
    only = lambda j, s: (0, 0, 0)

    sc = jnp.concatenate([jnp.stack([section, *chip_bits().values()]), edge]).astype(jnp.int32)
    saved, given = [], []
    x, which = inputs, by_section
    for layer in range(2):
        mine = section == layer
        vec = jnp.where(mine, vectors, vectors_r)
        om = jnp.where(mine, omega, omega_r)
        normed, u, f, vals, st = forward_inputs(layer, sc, x, vec, w_qkv, w_qkv_r, tables, om, ids[0], which)
        st = lax.ppermute(st, "row", other_row)
        num, den = own_half(f, vals, ids)
        att, rden, mid, n2, act, gp, res = forward_outputs(
            layer, sc, num, den, f, x, st, ids[0], vec, (w_out, w_up, w_down, w_out_r, w_up_r, w_down_r), which
        )
        saved.append((sc, x, vec, om, which, normed, u, f, vals, st, att, rden, mid, n2, act, gp))
        x, which = res[None], only
        given.append([lax.ppermute(g, "section", swap) for g in (n2, att, normed, act)])
    outs = (saved[1][1][0], x[0])

    def to_owner(of_layer):
        mine = jnp.where(first, of_layer[0], of_layer[1])
        other = lax.ppermute(jnp.where(first, of_layer[1], of_layer[0]), "section", swap)
        return join(mine, other, section)[None]

    hidden = to_owner(outs)

    links = Links() if lax.axis_size("wide") == 8 else None
    flows = {
        name + str(layer): Flow(links, KINDS[name + str(layer)], layer)
        for layer in range(2)
        for name in "duq"
    }
    at_own = lambda i, s: (s, 0, 0)
    at_other = lambda i, s: (1 - s, 0, 0)
    at_first = lambda i, s: (0, 0, 0)
    at_unit = lambda i, s: (0, 0, i)
    grads = {1: (cotangent, at_own, cotangent, at_other)}
    parts, back, done = {}, {}, {}
    shown = []

    def tied(value):
        (value,) = after([value], shown)
        shown.clear()
        return value

    def members(name):
        layer = int(name[1])
        normed, att, n2, act = (saved[layer][i] for i in (5, 10, 13, 14))
        gave_n2, gave_att, gave_normed, gave_act = given[layer]
        if name[0] == "d":
            left = (act, lambda i, s: (s, 0, i), gave_act, lambda i, s: (s, 0, i))
            return [(*left, *grads[layer], ff // UNIT)]

        def one(own, other, right, units):
            return (
                own[None], lambda i, s: (0, 0, s), other[None], lambda i, s: (0, 0, s),
                right[0][None], at_unit, right[1][None], at_unit, units,
            )

        if name[0] == "u":
            return [
                one(n2, gave_n2, done["up", layer], ff // UNIT),
                one(att, gave_att, done["br", layer], 1),
            ]
        return [one(normed, gave_normed, done["proj", layer], 3)]

    def run(item):
        name, layer = item[:2], int(item[1])
        if name in flows and len(item) == 2:
            before = list(shown)
            shown.clear()
            shown.extend(flows[name].advance(before))
        elif name in flows:
            send, keep = weight_grad(tied(sc), members(name), flows[name].first_dims())
            shown.append(send)
            flows[name].begin(send, keep)
        elif name[0] == "f":
            _, x, vec, om, which, normed, u, f, vals, st, att, rden, mid, n2, act, gp = saved[layer]
            g = grads[layer][0]
            back[layer] = ffn_back(
                layer, sc, g, tied(gp), mid, vec, att, rden, f, ids[0],
                (w_down, w_up, w_out, w_down_r, w_up_r, w_out_r),
                by_section if layer == 1 else only,
            )
            shown.append(back[layer][0])
            done["dst", layer] = lax.ppermute(back[layer][5], "row", other_row)
            done["up", layer] = both(back[layer][0])
            done["br", layer] = both(back[layer][2])
        elif name[0] == "a":
            _, x, vec, om, which, normed, u, f, vals, st = saved[layer][:10]
            d_mid, _, d_num, d_den = back[layer][1:5]
            out = attention_back(
                layer, sc, f, vals, tied(d_num), d_den, u, st, done["dst", layer], ids, tables, om,
                (x, vec, d_mid, w_qkv, w_qkv_r, which) if layer == 1 else None,
            )
            shown.append(out[0])
            done["proj", layer] = both(out[0])
            parts[layer] = out[1]
            if layer == 1:
                done["in", 1] = out[2:]
                own, other = both(out[2])
                grads[0] = (own[None], at_first, other[None], at_first)
        elif name[0] == "i":
            _, x, vec, om, which = saved[layer][:5]
            done["in", 0] = inputs_back(
                layer, sc, tied(done["proj", 0][0]), x, vec, back[0][1], w_qkv, w_qkv_r, which
            )
            shown.append(done["in", 0][0])
        elif name[0] == "s":
            smalls = []
            for k in range(2):
                s_bd, s_bu, s_g2, s_b2, s_bo = back[k][6:]
                smalls += [*done["in", k][1:], parts[k], s_bo, s_g2, s_b2, s_bu, s_bd]
            done["small"] = lax.psum(tied(pack(smalls)), ("section", "row", "wide"))
        else:
            kind, start, units, by_row = MATRICES[name]
            firsts, seconds = flows[kind + "0"].result, flows[kind + "1"].result
            dims = [flows[kind + str(k)].first_dims() for k in range(2)]
            done[name] = finish(tied(sc), firsts, seconds, start, units, by_row, dims)
            shown.append(done[name])

    token, fenced = jnp.zeros((8, LANES), F32), False
    for item in ORDER if links is not None else PLAIN:
        run(item)
        fenced = fenced or item == LAST
        if fenced and links is not None:
            token = fence(token, shown)
            shown[:] = [token]
    both_layers = done["small"].reshape(2, -1) + token[:1, :1]
    small = lax.dynamic_slice_in_dim(both_layers, section, 1)
    input_grads = to_owner((done["in", 0][0], done["in", 1][0]))
    g1, b1, bq, bo, gain2, bias2, bu, bd = cut(small, d, ff)
    return (
        hidden, input_grads, g1, b1, done["m0"], bq, done["m1"], bo,
        gain2, bias2, done["m2"], bu, done["m3"], bd,
    )


MATRICES = {"m0": ("q", 0, 3, False), "m1": ("u", 4, 1, False), "m2": ("u", 0, 4, False), "m3": ("d", 0, 4, True)}

KINDS = {
    "d1": ("yxwz", "xyzw"),
    "u1": ("xzwy", "zywx"),
    "q1": ("wyxz", "yxzw"),
    "d0": ("yxzw", "xywz"),
    "u0": ("xyzw", "yxwz"),
    "q0": ("yxwz", "xyzw"),
}

ORDER = (
    "f1", "d1w", "a1", "d1", "u1w", "d1", "d0w", "f0", "d0", "d1", "q1w", "d0", "a0", "u1", "u0w", "d0", "u1",
    "q0w", "q1", "u0", "i0", "d1", "q0", "q1", "u0", "d0", "s0", "d1", "q1", "d0", "u0", "u1", "d1", "q0",
    "q1", "d0", "u1", "u0", "q0", "u1", "q1", "u0", "q0", "d1", "d0", "m3", "q0", "u1", "u0", "q1", "u1",
    "u0", "m1", "q1", "q0", "m2", "q0", "m0",
)

LAST = "i0"

PLAIN = (
    "d1w", "d1", "f1", "u1w", "u1", "a1", "q1w", "q1", "d0w", "d0", "f0", "u0w", "u0", "a0", "q0w", "q0",
    "i0", "s0", "m3", "m2", "m1", "m0",
)


def cut(vec, d, ff):
    out, at = [], 0
    for size in (d, d, 3 * d, d, d, d, ff, d):
        out.append(vec[:, at : at + size])
        at += size
    return out


def solution(mesh):
    return jax.shard_map(
        local,
        mesh=mesh,
        in_specs=(
            P("wide", "row", None),
            P("wide", "row", None),
            P("wide", None),
            P(),
            P(),
            P(),
            P("section", None),
            P("section", None),
            P("section", None, None),
            P("section", None),
            P("section", None, None),
            P("section", None),
            P("section", None),
            P("section", None),
            P("section", None, None),
            P("section", None),
            P("section", None, None),
            P("section", None),
            P("section", None, None, None),
        ),
        out_specs=(
            P("section", "wide", "row", None),
            P("section", "wide", "row", None),
            P("section", None),
            P("section", None),
            P("section", None, None),
            P("section", None),
            P("section", None, None),
            P("section", None),
            P("section", None),
            P("section", None),
            P("section", None, None),
            P("section", None),
            P("section", None, None),
            P("section", None),
        ),
        check_vma=False,
    )
```
